32 devices in a mesh: pair: 16 (over z, x, core), trow: 2 (over y).
Axes of the slice: x: 2, y: 2, z: 4, core: 2. Of those that a mesh axis runs over, the one named last changes fastest.
Arguments:
- query_bank: bfloat16 [16, 64, 1024], P('pair'), may hold values from -6 to 6
- ref_owner: int32 [1], replicated, may hold values from 0 to 15
- target_feat: bfloat16 [16, 512, 1024], P('pair', None, 'trow'), may hold values from -60 to 60
- valid_rows: int32 [16], P('pair'), may hold values from 2 to 16, as said below
- w_first: bfloat16 [16, 1, 3, 3, 3, 3], replicated, may hold values from -2 to 2
- b_first: float32 [16], replicated, may hold values from -0.5 to 0.5
- w_middle: bfloat16 [16, 16, 3, 3, 3, 3], replicated, may hold values from -0.25 to 0.25
- b_middle: float32 [16], replicated, may hold values from -0.5 to 0.5
- w_last: bfloat16 [1, 16, 3, 3, 3, 3], replicated, may hold values from -0.25 to 0.25
- b_last: float32 [1], replicated, may hold values from -0.5 to 0.5
Outputs:
- scores: float32 [16, 64, 512], P('pair', None, 'trow')
The draws below stay inside these ranges and needn't reach their ends.
Inputs may be any that keep to these rules, and one draw needn't show every extreme that they name: ref_owner names the group along pair whose window is the reference. Rows of a target grid at or past valid_rows are padding; some pair fills all 16 rows.
All inputs are finite; a program needn't handle non-finite values.
Results may differ from the reference program's by a relative error of at most 0.007.
Values may be sent and summed in bfloat16 or wider, within the bound.
No kernel may reach another device: no remote copies, remote signals or barrier semaphores. Data moves between devices by JAX's collectives and lax.ppermute only.
A program may use at most 64 MiB of HBM per device.

```python
import math
import jax
import jax.numpy as jnp
from jax import lax

C = 1024
CH = 16
HB = 16
WB = 32
WA = 32
GROUPS = 16
PAIRS = 16
NA = 64
NB = 512


def draw_target_feat(key, part):
    key_base = jax.random.fold_in(key, 11)
    key_scale = jax.random.fold_in(key, 12)
    row_scale = jnp.exp(jax.random.uniform(key_scale, (PAIRS, NB, 1), jnp.float32, 0.0, math.log(10.0)))
    samples = jax.random.normal(key_base, (PAIRS, NB, C), jnp.float32) * row_scale
    return jnp.clip(samples, -60.0, 60.0).astype(jnp.bfloat16)


def draw_valid_rows(key, part):
    key_rows = jax.random.fold_in(key, 21)
    key_spot = jax.random.fold_in(key, 22)
    counts = jax.random.randint(key_rows, (PAIRS,), 2, HB + 1)
    chosen = jax.random.randint(key_spot, (2,), 0, PAIRS)
    position = jnp.arange(PAIRS)
    counts = jnp.where(position == chosen[0], HB, counts)
    counts = jnp.where((position == chosen[1]) & (chosen[1] != chosen[0]), 2, counts)
    return counts.astype(jnp.int32)


def levels(stream_key, shape, split, smallest, high):
    level, own = 1.0, jax.random.fold_in(stream_key, 6)
    for dim, blocks in split:
        steps = jnp.exp(jax.random.uniform(jax.random.fold_in(own, dim), (blocks,), jnp.float32, smallest / len(split), high / len(split)))
        level = level * jnp.repeat(steps, shape[dim] // blocks).reshape([-1 if axis == dim else 1 for axis in range(len(shape))])
    return level


def scatter_about(stream_key, dims, scale, most, pieces=(), kind=jnp.bfloat16):
    level = levels(stream_key, dims, pieces, -0.22, 0.18) if pieces else 1.0
    entries = jax.random.normal(stream_key, dims, jnp.float32) * scale * level
    return jnp.minimum(jnp.maximum(entries, -most), most).astype(kind)


def setup_inputs(seed: int = 0) -> dict:
    splits = jax.random.split(jax.random.key(seed), 11)
    query_bank = scatter_about(splits[0], (GROUPS, NA, C), 1.0, 6.0, ((0, 16),))
    ref_owner = jax.random.randint(splits[1], (1,), 0, GROUPS).astype(jnp.int32)
    target_feat = draw_target_feat(jax.random.fold_in(splits[10], 71), 0)
    valid_rows = draw_valid_rows(jax.random.fold_in(splits[10], 71), 0)
    w_first = scatter_about(splits[4], (CH, 1, 3, 3, 3, 3), 9 ** -0.5, 2.0)
    b_first = jnp.clip(jax.random.uniform(splits[5], (CH,), jnp.float32, -0.5, 0.5), -0.5, 0.5)
    w_middle = scatter_about(splits[6], (CH, CH, 3, 3, 3, 3), (81 * CH // 2) ** -0.5, 0.25)
    b_middle = jnp.clip(jax.random.uniform(splits[7], (CH,), jnp.float32, -0.5, 0.5), -0.5, 0.5)
    w_last = scatter_about(splits[8], (1, CH, 3, 3, 3, 3), (81 * CH // 2) ** -0.5, 0.25)
    b_last = jnp.clip(jax.random.uniform(splits[9], (1,), jnp.float32, -0.5, 0.5), -0.5, 0.5)
    return dict(query_bank=query_bank, ref_owner=ref_owner, target_feat=target_feat, valid_rows=valid_rows, w_first=w_first, b_first=b_first, w_middle=w_middle, b_middle=b_middle, w_last=w_last, b_last=b_last)


EPS_NORM = 1e-06
EPS_PEAK = 1e-05

def shift_along(values, offset, axis_dim):
    if offset == 0:
        return values
    length = values.shape[axis_dim]
    zero_shape = list(values.shape)
    zero_shape[axis_dim] = abs(offset)
    zero_block = jnp.zeros(zero_shape, values.dtype)
    if offset > 0:
        return jnp.concatenate([lax.slice_in_dim(values, offset, length, axis=axis_dim), zero_block], axis=axis_dim)
    return jnp.concatenate([zero_block, lax.slice_in_dim(values, 0, length + offset, axis=axis_dim)], axis=axis_dim)

def block_conv(row_block, weight_matrix, out_channels, block_rows, exact):
    extent = row_block.shape[2]
    column_pos = jnp.arange(extent, dtype=jnp.int32) % WB
    shifted = []
    for col_off in (-1, 0, 1):
        in_range = (column_pos + col_off >= 0) & (column_pos + col_off < WB)
        moved_cols = shift_along(row_block, col_off, 2)
        shifted.append(jnp.where(in_range[None, None, :], moved_cols, jnp.zeros((), row_block.dtype)))
    layers = []
    for row_off in range(3):
        for col_idx in range(3):
            layers.append(lax.slice_in_dim(shifted[col_idx], row_off * WB, (row_off + block_rows) * WB, axis=2))
    stacked = jnp.concatenate(layers, axis=0)
    if exact:
        products = jnp.einsum('pk,kab->pab', weight_matrix.astype(jnp.float32), stacked.astype(jnp.float32))
    else:
        products = jnp.einsum('pk,kab->pab', weight_matrix, stacked, preferred_element_type=jnp.float32)
    positions = row_block.shape[1]
    query_row = jnp.arange(positions, dtype=jnp.int32) // WA
    query_col = jnp.arange(positions, dtype=jnp.int32) % WA
    ref_rows = positions // WA
    accumulated = jnp.zeros((out_channels, positions, block_rows * WB), jnp.float32)
    for row_off in range(3):
        for col_off in range(3):
            start_chan = (row_off * 3 + col_off) * out_channels
            offset_group = products[start_chan:start_chan + out_channels]
            in_range = (query_row + row_off - 1 >= 0) & (query_row + row_off - 1 < ref_rows)
            in_range = in_range & (query_col + col_off - 1 >= 0) & (query_col + col_off - 1 < WA)
            moved_group = shift_along(offset_group, (row_off - 1) * WA + col_off - 1, 1)
            accumulated = accumulated + jnp.where(in_range[None, :, None], moved_group, 0.0)
    return accumulated

def conv_layer(inputs, weight, bias, exact):
    out_channels = weight.shape[0]
    in_channels = weight.shape[1]
    weight_matrix = jnp.transpose(weight, (2, 3, 0, 4, 5, 1)).reshape(9 * out_channels, 9 * in_channels)
    rows_out = inputs.shape[2] // WB - 2
    block_rows = 1
    for option in (2, 4):
        if rows_out % option == 0:
            block_rows = option

    def one_block(block_index):
        row_block = lax.dynamic_slice_in_dim(inputs, block_index * (block_rows * WB), (block_rows + 2) * WB, 2)
        return block_conv(row_block, weight_matrix, out_channels, block_rows, exact)
    block_outputs = lax.map(one_block, jnp.arange(rows_out // block_rows, dtype=jnp.int32))
    joined = jnp.transpose(block_outputs, (1, 2, 0, 3)).reshape(out_channels, inputs.shape[1], rows_out * WB)
    return joined + bias[:, None, None]

def unit_rows(features):
    values = features.astype(jnp.float32)
    return (values * lax.rsqrt(lax.optimization_barrier(jnp.sum(values * values, axis=1, keepdims=True)) + EPS_NORM)).astype(jnp.bfloat16)

def contract(left, right):
    return lax.dot_general(left, right, (((1,), (1,)), ((), ())), preferred_element_type=jnp.float32)

def reference(query_bank, ref_owner, target_feat, valid_rows, w_first, b_first, w_middle, b_middle, w_last, b_last):
    query_vec = lax.dynamic_index_in_dim(query_bank, ref_owner[0], 0, keepdims=False)
    unit_query = unit_rows(query_vec)
    cos_scale = math.sqrt(query_bank.shape[2])
    global_row = jnp.arange(HB * WB, dtype=jnp.int32) // WB

    def one_pair(pair_item):
        target, row_count = pair_item
        raw_dot = contract(unit_query, target)
        squares = lax.optimization_barrier(jnp.sum(jnp.square(target.astype(jnp.float32)), axis=1))
        is_live = global_row < row_count
        correlation = jnp.where(is_live[None, :], cos_scale * raw_dot * lax.rsqrt(squares + EPS_NORM)[None, :], 0.0)
        magnitude = jnp.abs(correlation)
        peak_query = lax.optimization_barrier(jnp.max(magnitude, axis=0))
        peak_target = lax.optimization_barrier(jnp.max(magnitude, axis=1))
        volume = correlation * (correlation / (peak_query[None, :] + EPS_PEAK)) * (correlation / (peak_target[:, None] + EPS_PEAK))
        volume = volume.astype(jnp.bfloat16)[None]
        padded = jnp.pad(volume, ((0, 0), (0, 0), (WB, WB)))
        hidden = jnp.maximum(conv_layer(padded, w_first, b_first, True), 0.0).astype(jnp.bfloat16)
        padded = jnp.pad(hidden, ((0, 0), (0, 0), (WB, WB)))
        hidden = jnp.maximum(conv_layer(padded, w_middle, b_middle, True), 0.0).astype(jnp.bfloat16)
        padded = jnp.pad(hidden, ((0, 0), (0, 0), (WB, WB)))
        result = conv_layer(padded, w_last, b_last, True)[0]
        return jnp.where(is_live[None, :], result, 0.0)
    return lax.map(one_pair, (target_feat, valid_rows))
```

```python
import functools
import math

import jax
import jax.numpy as jnp
from jax import lax
from jax.experimental import pallas as pl
from jax.experimental.pallas import tpu as pltpu
from jax.sharding import PartitionSpec as P

WB = 32
WA = 32

EPS_NORM = 1e-06
EPS_PEAK = 1e-05

F32 = jnp.float32
BF16 = jnp.bfloat16
NT = (((1,), (1,)), ((), ()))
PITCH = WB + 8
VMEM_LIMIT = 48 * 1024 * 1024


def swapped(values, axis, distance):
    count = lax.axis_size(axis)
    return lax.ppermute(values, axis, [(i, i ^ distance) for i in range(count)])


def spread(window, owner, axis):
    count = lax.axis_size(axis)
    rank = lax.axis_index(axis)
    held = jnp.where(rank == owner, window, jnp.zeros_like(window))
    half = window.shape[0] // 2
    bit = rank % 2
    keep = lax.dynamic_slice_in_dim(held, bit * half, half, 0)
    give = lax.dynamic_slice_in_dim(held, (1 - bit) * half, half, 0)
    held = keep + swapped(give, axis, 1)
    bits = [1 << b for b in range(1, count.bit_length() - 1)]
    rounds = []
    if len(bits) % 2:
        rounds.append(bits[:1])
        bits = bits[1:]
    for at in range(0, len(bits), 2):
        low, high = bits[at : at + 2]
        rounds.append([low, high, low + high])
    for distances in rounds:
        held = held + sum(swapped(held, axis, d) for d in distances)
    return held, swapped(held, axis, 1)


def dot(left, right):
    return jnp.dot(left, right, preferred_element_type=F32)


def dot_nt(left, right):
    return lax.dot_general(left, right, NT, preferred_element_type=F32)


def iota(shape, dim):
    return lax.broadcasted_iota(jnp.int32, shape, dim)


def one_hot(cond):
    return jnp.where(cond, 1.0, 0.0).astype(BF16)


def expand_kernel(ch, wf_ref, wm_ref, wl_ref, w1_ref, w2_ref, w3_ref):
    group = 2 * ch
    index = lambda i, j, k, l: ((i * 3 + j) * 3 + k) * 3 + l

    taps = wf_ref[...]
    lane = iota((81, 128), 1)
    src = iota((81, 128), 0)
    base = []
    for k in range(3):
        for ra in range(2):
            l, rp, j = lane // 6, (lane // 3) % 2, lane % 3
            want = (((rp - ra + 1) * 3 + j) * 3 + k) * 3 + l
            base.append(dot(taps, one_hot((src == want) & (lane < 18))))
    base = jnp.concatenate(base, axis=0).astype(BF16)
    row = iota((128, 256), 0)
    col = iota((128, 256), 1)
    l, rp, j = row // 6, (row // 3) % 2, row % 3
    for ca in range(WA):
        at = ca + j - 1
        place = one_hot((col == l * 64 + rp * WA + at) & (at >= 0) & (at < WA) & (row < 18))
        block = dot(base, place).astype(BF16)
        for k in range(3):
            w1_ref[k, ca * group : (ca + 1) * group, :] = block[k * group : (k + 1) * group]

    total = None
    row = iota((ch, 128), 0)
    col = iota((ch, 128), 1)
    for j in range(3):
        for rp in range(2):
            picked = jnp.concatenate(
                [wm_ref[index(rp - ra + 1, j, k, l)] for k in range(3) for l in range(3) for ra in range(2)],
                axis=0,
            )
            part = dot(picked, one_hot(col == j * group + rp * ch + row))
            total = part if total is None else total + part
    base = total.astype(BF16)
    row = iota((128, 256), 0)
    col = iota((128, 256), 1)
    moves = [one_hot((col == row + group * b) & (row < 3 * group)) for b in range(4)]
    moved = [dot(base, m).astype(BF16) for m in moves]
    blank = jnp.zeros((group, 128), BF16)
    for tap in range(9):
        for ca in range(8):
            a, b = divmod(ca + 3, 4)
            piece = moved[b][tap * group : (tap + 1) * group]
            for v in range(4):
                chunk = piece[:, :128] if v == a else piece[:, 128:] if v == a + 1 else blank
                w2_ref[tap, ca * group : (ca + 1) * group, v * 128 : (v + 1) * 128] = chunk

    taps = wl_ref[...]
    out_row = iota((24, 81), 0)
    src = iota((24, 81), 1)
    row = iota((ch, 128), 0)
    col = iota((ch, 128), 1)
    total = None
    for j in range(3):
        for rp in range(2):
            k, l, ra = out_row // 8, (out_row % 8) // 2, out_row % 2
            want = (((rp - ra + 1) * 3 + j) * 3 + k) * 3 + l
            picked = dot(one_hot((src == want) & (l < 3)), taps).astype(BF16)
            part = dot(picked, one_hot(col == j * group + rp * ch + row))
            total = part if total is None else total + part
    base = total.astype(BF16)
    moved = [dot(base, m) for m in moves]
    blank = jnp.zeros((8, 128), F32)
    lanes = WA * group // 128
    for k in range(3):
        for pair in range(WA // 2):
            for v in range(lanes):
                chunks = []
                for ca in (2 * pair, 2 * pair + 1):
                    a, b = (ca - 1) // 4, (ca - 1) % 4
                    piece = moved[b][k * 8 : (k + 1) * 8]
                    chunks.append(piece[:, :128] if v == a else piece[:, 128:] if v == a + 1 else blank)
                w3_ref[k, pair * 16 : (pair + 1) * 16, v * 128 : (v + 1) * 128] = jnp.concatenate(
                    chunks, axis=0
                ).astype(BF16)


def score_kernel(
    rows_here, n1, n2, s_ref, b3_ref, tm_ref, to_ref, qa_ref, qb_ref, w1_ref, w2_ref, w3_ref, b1_ref, b2_ref,
    out_ref, v_ref, x_ref, h1_ref, h2_ref, ya_ref, yb_ref, yt_ref,
):
    count, trow, bit = s_ref[0], s_ref[1], s_ref[2]
    cells = tm_ref.shape[0]
    grid_rows = cells // WB
    width = tm_ref.shape[1]
    scale = math.sqrt(2 * width)
    start1 = jnp.clip(rows_here * trow - 2, 0, grid_rows - n1)
    start2 = jnp.clip(rows_here * trow - 1, 0, grid_rows - n2)

    def unit(ref):
        values = ref[...].astype(F32)
        return (values * lax.rsqrt(jnp.sum(values * values, axis=1, keepdims=True) + EPS_NORM)).astype(BF16)

    qa, qb = unit(qa_ref), unit(qb_ref)
    own_first = bit == 0
    q0 = jnp.where(own_first, qa, qb)
    q1 = jnp.where(own_first, qb, qa)
    query = jnp.concatenate([q0, q1, q0, q1], axis=0)
    low, high = query[:, :width], query[:, width:]
    near = jnp.where(trow == 0, low, high)
    far = jnp.where(trow == 0, high, low)
    raw = dot_nt(tm_ref[...], near) + dot_nt(to_ref[...], far)

    def squares(ref):
        values = ref[...].astype(F32)
        return jnp.sum(values * values, axis=1, keepdims=True)

    inv = lax.rsqrt(squares(tm_ref) + squares(to_ref) + EPS_NORM)
    live = iota((cells, 128), 0) // WB < count
    corr = jnp.where(live, scale * raw * inv, 0.0)
    mag = jnp.abs(corr)
    peak_query = jnp.max(mag, axis=1, keepdims=True)
    peak_target = jnp.max(mag, axis=0, keepdims=True)
    volume = corr * (corr * (1.0 / (peak_query + EPS_PEAK))) * (corr * (1.0 / (peak_target + EPS_PEAK)))

    v_ref[0 : 8 + PITCH, :] = jnp.zeros((8 + PITCH, 128), F32)
    v_ref[8 + (grid_rows + 1) * PITCH :, :] = jnp.zeros((PITCH, 128), F32)
    for r in range(grid_rows):
        at = 8 + (r + 1) * PITCH
        v_ref[at : at + WB, :] = volume[r * WB : (r + 1) * WB]
        v_ref[at + WB : at + PITCH, :] = jnp.zeros((PITCH - WB, 128), F32)

    half = WB // 2
    left = iota((half, 128), 1) < 64
    for r in range(n1 + 2):
        at = pl.multiple_of((start1 + r) * PITCH, 8)
        slabs = [v_ref[pl.ds(at + 8 + o, half, stride=2), :] for o in (-1, 0, 1, 2)]
        for u in range(2):
            x_ref[r, u * half : (u + 1) * half, 0:128] = jnp.where(left, slabs[u], slabs[u + 1]).astype(BF16)
            x_ref[r, u * half : (u + 1) * half, 128:256] = jnp.where(left, slabs[u + 2], 0.0).astype(BF16)

    lanes = h1_ref.shape[2]
    zero = jnp.zeros((2 * WB, lanes), BF16)
    h1_ref[0] = zero
    h1_ref[n1 + 1] = zero
    h2_ref[0] = zero[:WB]
    h2_ref[n2 + 1] = zero[:WB]
    step = iota((n1 * half, 256), 0) % half
    for q in range(lanes // 256):
        cols = slice(q * 256, (q + 1) * 256)
        total = b1_ref[:, cols]
        for k in range(3):
            total = total + dot_nt(x_ref[k : k + n1].reshape(n1 * WB, 256), w1_ref[k, cols, :])
        total = jnp.maximum(total, 0.0)
        h1_ref[1 : n1 + 1, half : half + WB, cols] = total.reshape(n1, WB, 256).astype(BF16)
        parts = total.reshape(n1, 2, half, 256)
        even = parts[:, 0].reshape(n1 * half, 256)
        odd = parts[:, 1].reshape(n1 * half, 256)
        before = jnp.where(step == 0, 0.0, pltpu.roll(odd, 1, 0))
        after = jnp.where(step == half - 1, 0.0, pltpu.roll(even, n1 * half - 1, 0))
        h1_ref[1 : n1 + 1, 0:half, cols] = before.reshape(n1, half, 256).astype(BF16)
        h1_ref[1 : n1 + 1, half + WB :, cols] = after.reshape(n1, half, 256).astype(BF16)

    off2 = start2 - start1
    for q in range(lanes // 256):
        cols = slice(q * 256, (q + 1) * 256)
        lo, hi = max(q * 256 - 128, 0), min(q * 256 + 384, lanes)
        total = b2_ref[:, cols]
        for k in range(3):
            for l in range(3):
                cells_in = h1_ref[pl.ds(off2 + k, n2), l * half : l * half + WB, lo:hi].reshape(n2 * WB, hi - lo)
                total = total + dot_nt(cells_in, w2_ref[k * 3 + l, :, lo - q * 256 + 128 : hi - q * 256 + 128])
        h2_ref[1 : n2 + 1, :, cols] = jnp.maximum(total, 0.0).reshape(n2, WB, 256).astype(BF16)

    off3 = rows_here * trow - start2
    total = None
    for k in range(3):
        part = dot_nt(h2_ref[pl.ds(off3 + k, rows_here)].reshape(rows_here * WB, lanes), w3_ref[k])
        total = part if total is None else total + part
    for r in range(rows_here):
        for u in range(2):
            piece = total[(r * 2 + u) * half : (r * 2 + u + 1) * half]
            ya_ref[pl.ds(r * WB + u, half, stride=2), :] = piece[:, :128]
            yb_ref[pl.ds(r * WB + u, half, stride=2), :] = piece[:, 128:]
    here = rows_here * WB
    for v in range(here // 128):
        yt_ref[v, 0:128, :] = ya_ref[v * 128 : (v + 1) * 128, :].T
        yt_ref[v, 128:256, :] = yb_ref[v * 128 : (v + 1) * 128, :].T
    lane = iota((WA, here), 1)
    keep = rows_here * trow + lane // WB < count
    for ra in range(2):
        parts = [
            jnp.concatenate([yt_ref[v, pl.ds(l * 2 + ra, WA, stride=8), :] for v in range(here // 128)], axis=1)
            for l in range(3)
        ]
        before = jnp.where(lane % WB == 0, 0.0, pltpu.roll(parts[0], 1, 1))
        after = jnp.where(lane % WB == WB - 1, 0.0, pltpu.roll(parts[2], here - 1, 1))
        result = before + parts[1] + after + b3_ref[0]
        out_ref[0, ra * WA : (ra + 1) * WA, :] = jnp.where(keep, result, 0.0)


def per_device(
    query_bank, ref_owner, target_feat, valid_rows, w_first, b_first, w_middle, b_middle, w_last, b_last
):
    target = target_feat[0]
    cells, width = target.shape
    positions = query_bank.shape[1]
    ch = w_middle.shape[0]
    group = 2 * ch
    lanes = WA * group
    trows = lax.axis_size("trow")
    grid_rows = cells // WB
    rows_here = grid_rows // trows
    sides = 1 if trows == 2 else 2
    n1, n2 = min(rows_here + 2 * sides, grid_rows), min(rows_here + sides, grid_rows)

    other = swapped(target, "trow", 1)
    own, sibling = spread(query_bank[0], ref_owner[0], "pair")
    scalars = jnp.stack([valid_rows[0], lax.axis_index("trow"), lax.axis_index("pair") % 2]).astype(jnp.int32)

    vmem = pl.BlockSpec(memory_space=pltpu.VMEM)
    smem = pl.BlockSpec(memory_space=pltpu.SMEM)
    w1, w2, w3 = pl.pallas_call(
        functools.partial(expand_kernel, ch),
        out_shape=(
            jax.ShapeDtypeStruct((3, lanes, 256), BF16),
            jax.ShapeDtypeStruct((9, 256, 512), BF16),
            jax.ShapeDtypeStruct((3, 256, lanes), BF16),
        ),
        in_specs=[vmem] * 3,
        out_specs=(vmem,) * 3,
        compiler_params=pltpu.CompilerParams(vmem_limit_bytes=VMEM_LIMIT),
        name="expand",
    )(
        w_first.reshape(ch, 81),
        jnp.transpose(w_middle, (2, 3, 4, 5, 0, 1)).reshape(81, ch, ch),
        jnp.transpose(w_last[0], (1, 2, 3, 4, 0)).reshape(81, ch),
    )
    b1 = jnp.tile(b_first, lanes // ch)[None]
    b2 = jnp.tile(b_middle, lanes // ch)[None]

    return pl.pallas_call(
        functools.partial(score_kernel, rows_here, n1, n2),
        out_shape=jax.ShapeDtypeStruct((1, positions, rows_here * WB), F32),
        in_specs=[smem, smem] + [vmem] * 9,
        out_specs=vmem,
        scratch_shapes=[
            pltpu.VMEM((8 + (grid_rows + 2) * PITCH, 128), F32),
            pltpu.VMEM((n1 + 2, WB, 256), BF16),
            pltpu.VMEM((n1 + 2, 2 * WB, lanes), BF16),
            pltpu.VMEM((n2 + 2, WB, lanes), BF16),
            pltpu.VMEM((rows_here * WB, 128), F32),
            pltpu.VMEM((rows_here * WB, 128), F32),
            pltpu.VMEM((rows_here * WB // 128, 256, 128), F32),
        ],
        compiler_params=pltpu.CompilerParams(vmem_limit_bytes=VMEM_LIMIT),
        name="score",
    )(scalars, b_last, target, other, own, sibling, w1, w2, w3, b1, b2)


def solution(mesh):
    in_specs = (
        P("pair", None, None),
        P(),
        P("pair", None, "trow"),
        P("pair"),
        P(),
        P(),
        P(),
        P(),
        P(),
        P(),
    )
    out_specs = P("pair", None, "trow")
    return jax.shard_map(per_device, mesh=mesh, in_specs=in_specs, out_specs=out_specs, check_vma=False)
```

```python
import functools
import math

import jax
import jax.numpy as jnp
from jax import lax
from jax.experimental import pallas as pl
from jax.experimental.pallas import tpu as pltpu
from jax.sharding import PartitionSpec as P

WB = 32
WA = 32

EPS_NORM = 1e-06
EPS_PEAK = 1e-05

F32 = jnp.float32
BF16 = jnp.bfloat16
NT = (((1,), (1,)), ((), ()))
PITCH = WB + 8
VMEM_LIMIT = 16 * 1024 * 1024
VMEM = pl.BlockSpec(memory_space=pltpu.VMEM)
SMEM = pl.BlockSpec(memory_space=pltpu.SMEM)
HBM = pl.BlockSpec(memory_space=pltpu.HBM)


def swapped(values, axis, distance):
    count = lax.axis_size(axis)
    return lax.ppermute(values, axis, [(i, i ^ distance) for i in range(count)])


def front_kernel(rank_ref, window_hbm, keep_ref, give_ref, sems):
    half = keep_ref.shape[0]
    bit = rank_ref[0] % 2
    copies = [
        pltpu.make_async_copy(window_hbm.at[pl.ds(pl.multiple_of(which * half, half), half)], ref, sems.at[n])
        for n, (which, ref) in enumerate(((bit, keep_ref), (1 - bit, give_ref)))
    ]
    for copy in copies:
        copy.start()
    for copy in copies:
        copy.wait()


def spread(window, owner, axis):
    count = lax.axis_size(axis)
    rank = lax.axis_index(axis)
    half = jax.ShapeDtypeStruct((window.shape[0] // 2, window.shape[1]), window.dtype)
    keep, give = pl.pallas_call(
        front_kernel,
        out_shape=(half, half),
        in_specs=[SMEM, HBM],
        out_specs=(VMEM, VMEM),
        scratch_shapes=[pltpu.SemaphoreType.DMA((2,))],
        compiler_params=pltpu.CompilerParams(vmem_limit_bytes=VMEM_LIMIT),
        name="front",
    )(rank.reshape(1), in_hbm(window))
    held = jnp.where(rank == owner, keep, swapped(give, axis, 1))
    held = jnp.where(rank // 2 == owner // 2, held, jnp.zeros_like(held))
    bits = [1 << b for b in range(1, count.bit_length() - 1)]
    rounds = []
    if len(bits) % 2:
        rounds.append(bits[:1])
        bits = bits[1:]
    for at in range(0, len(bits), 2):
        low, high = bits[at : at + 2]
        rounds.append([low, high, low + high])
    for distances in rounds:
        held = held + sum(swapped(held, axis, d) for d in distances)
    return held, swapped(held, axis, 1)


def in_hbm(array):
    return pltpu.with_memory_space_constraint(array, pltpu.HBM)


def dot(left, right):
    return jnp.dot(left, right, preferred_element_type=F32)


def dot_nt(left, right):
    return lax.dot_general(left, right, NT, preferred_element_type=F32)


def iota(shape, dim):
    return lax.broadcasted_iota(jnp.int32, shape, dim)


def one_hot(cond):
    return jnp.where(cond, 1.0, 0.0).astype(BF16)


def expand_kernel(
    ch, misc_ref, wf_hbm, wm_hbm, wl_hbm, w1_ref, w2_ref, w3_ref, rows_ref, wf_ref, wm_ref, wl_ref, sems
):
    group = 2 * ch
    pairs = ((wf_hbm, wf_ref), (wm_hbm, wm_ref), (wl_hbm, wl_ref))
    copies = [pltpu.make_async_copy(src, dst, sems.at[n]) for n, (src, dst) in enumerate(pairs)]
    for copy in copies:
        copy.start()

    misc = misc_ref[...]
    chan = iota((8, 128), 1)
    for n in range(2):
        total = jnp.where(chan < ch, pltpu.roll(misc, 128 - n * ch, 1) if n else misc, 0.0)
        size = ch
        while size < 128:
            total = total + pltpu.roll(total, size, 1)
            size *= 2
        rows_ref[n : n + 1, 0:128] = total[0:1]
        rows_ref[n : n + 1, 128:256] = total[0:1]
    for n in range(2):
        at = 2 * ch + n
        rows_ref[2 + n : 3 + n, :] = jnp.broadcast_to(misc[0:1, at : at + 1], (1, 256))

    for copy in copies:
        copy.wait()

    def by_offset(ref):
        values = ref[...].astype(F32)
        fill = jnp.zeros((32 - values.shape[0], ch), F32)
        return jnp.concatenate([part for l in range(3) for part in (values[:, l, :], fill)], axis=0)

    taps = by_offset(wf_ref)
    taps = jnp.concatenate([taps, jnp.zeros((32, ch), F32)], axis=0)
    taps = jnp.concatenate([taps, jnp.zeros((128, 128 - ch), F32)], axis=1).T[:ch].astype(BF16)
    lane = iota((128, 128), 1)
    src = iota((128, 128), 0)
    base = []
    for k in range(3):
        for ra in range(2):
            l, rp, j = lane // 6, (lane // 3) % 2, lane % 3
            want = l * 32 + ((rp - ra + 1) * 3 + j) * 3 + k
            base.append(dot(taps, one_hot((src == want) & (lane < 18))))
    base = jnp.concatenate(base, axis=0).astype(BF16)
    row = iota((128, 256), 0)
    col = iota((128, 256), 1)
    l, rp, j = row // 6, (row // 3) % 2, row % 3
    for ca in range(WA):
        at = ca + j - 1
        place = one_hot((col == l * 64 + rp * WA + at) & (at >= 0) & (at < WA) & (row < 18))
        block = dot(base, place).astype(BF16)
        for k in range(3):
            w1_ref[k, ca * group : (ca + 1) * group, :] = block[k * group : (k + 1) * group]

    total = None
    row = iota((ch, 128), 0)
    col = iota((ch, 128), 1)
    for j in range(3):
        for rp in range(2):
            picked = jnp.concatenate(
                [wm_ref[(((rp - ra + 1) * 3 + j) * 3 + k) * 3 + l] for k in range(3) for l in range(3) for ra in range(2)],
                axis=0,
            )
            part = dot(picked, one_hot(col == j * group + rp * ch + row))
            total = part if total is None else total + part
    base = total.astype(BF16)
    row = iota((128, 256), 0)
    col = iota((128, 256), 1)
    moves = [one_hot((col == row + group * b) & (row < 3 * group)) for b in range(4)]
    moved = [dot(base, m).astype(BF16) for m in moves]
    blank = jnp.zeros((group, 128), BF16)
    for tap in range(9):
        for ca in range(8):
            a, b = divmod(ca + 3, 4)
            piece = moved[b][tap * group : (tap + 1) * group]
            for v in range(4):
                chunk = piece[:, :128] if v == a else piece[:, 128:] if v == a + 1 else blank
                w2_ref[tap, ca * group : (ca + 1) * group, v * 128 : (v + 1) * 128] = chunk

    taps = by_offset(wl_ref).astype(BF16)
    out_row = iota((24, 96), 0)
    src = iota((24, 96), 1)
    row = iota((ch, 128), 0)
    col = iota((ch, 128), 1)
    total = None
    for j in range(3):
        for rp in range(2):
            k, l, ra = out_row // 8, (out_row % 8) // 2, out_row % 2
            want = l * 32 + ((rp - ra + 1) * 3 + j) * 3 + k
            picked = dot(one_hot((src == want) & (l < 3)), taps).astype(BF16)
            part = dot(picked, one_hot(col == j * group + rp * ch + row))
            total = part if total is None else total + part
    base = total.astype(BF16)
    moved = [dot(base, m) for m in moves]
    blank = jnp.zeros((8, 128), F32)
    lanes = WA * group // 128
    for k in range(3):
        for pair in range(WA // 2):
            for v in range(lanes):
                chunks = []
                for ca in (2 * pair, 2 * pair + 1):
                    a, b = (ca - 1) // 4, (ca - 1) % 4
                    piece = moved[b][k * 8 : (k + 1) * 8]
                    chunks.append(piece[:, :128] if v == a else piece[:, 128:] if v == a + 1 else blank)
                w3_ref[k, pair * 16 : (pair + 1) * 16, v * 128 : (v + 1) * 128] = jnp.concatenate(
                    chunks, axis=0
                ).astype(BF16)


def score_kernel(
    rows_here, n1, n2, s_ref, rows_ref, tm_ref, to_ref, qa_ref, qb_ref, w1_ref, w2_ref, w3_ref,
    out_ref, v_ref, x_ref, h1_ref, h2_ref, ya_ref, yb_ref, yt_ref,
):
    trow, bit = s_ref[0], s_ref[1]
    count = rows_ref[3:4, :]
    cells = tm_ref.shape[0]
    grid_rows = cells // WB
    width = tm_ref.shape[1]
    scale = math.sqrt(2 * width)
    start1 = jnp.clip(rows_here * trow - 2, 0, grid_rows - n1)
    start2 = jnp.clip(rows_here * trow - 1, 0, grid_rows - n2)

    def unit(ref):
        values = ref[...].astype(F32)
        return (values * lax.rsqrt(jnp.sum(values * values, axis=1, keepdims=True) + EPS_NORM)).astype(BF16)

    qa, qb = unit(qa_ref), unit(qb_ref)
    own_first = bit == 0
    q0 = jnp.where(own_first, qa, qb)
    q1 = jnp.where(own_first, qb, qa)
    query = jnp.concatenate([q0, q1, q0, q1], axis=0)
    low, high = query[:, :width], query[:, width:]
    near = jnp.where(trow == 0, low, high)
    far = jnp.where(trow == 0, high, low)
    raw = dot_nt(tm_ref[...], near) + dot_nt(to_ref[...], far)

    def squares(ref):
        values = ref[...].astype(F32)
        return jnp.sum(values * values, axis=1, keepdims=True)

    inv = lax.rsqrt(squares(tm_ref) + squares(to_ref) + EPS_NORM)
    live = (iota((cells, 128), 0) // WB).astype(F32) < count[:, :128]
    corr = jnp.where(live, scale * raw * inv, 0.0)
    mag = jnp.abs(corr)
    peak_query = jnp.max(mag, axis=1, keepdims=True)
    peak_target = jnp.max(mag, axis=0, keepdims=True)
    volume = corr * (corr * (1.0 / (peak_query + EPS_PEAK))) * (corr * (1.0 / (peak_target + EPS_PEAK)))

    v_ref[0 : 8 + PITCH, :] = jnp.zeros((8 + PITCH, 128), F32)
    v_ref[8 + (grid_rows + 1) * PITCH :, :] = jnp.zeros((PITCH, 128), F32)
    for r in range(grid_rows):
        at = 8 + (r + 1) * PITCH
        v_ref[at : at + WB, :] = volume[r * WB : (r + 1) * WB]
        v_ref[at + WB : at + PITCH, :] = jnp.zeros((PITCH - WB, 128), F32)

    half = WB // 2
    left = iota((half, 128), 1) < 64
    for r in range(n1 + 2):
        at = pl.multiple_of((start1 + r) * PITCH, 8)
        slabs = [v_ref[pl.ds(at + 8 + o, half, stride=2), :] for o in (-1, 0, 1, 2)]
        for u in range(2):
            x_ref[r, u * half : (u + 1) * half, 0:128] = jnp.where(left, slabs[u], slabs[u + 1]).astype(BF16)
            x_ref[r, u * half : (u + 1) * half, 128:256] = jnp.where(left, slabs[u + 2], 0.0).astype(BF16)

    lanes = h1_ref.shape[2]
    zero = jnp.zeros((2 * WB, lanes), BF16)
    h1_ref[0] = zero
    h1_ref[n1 + 1] = zero
    h2_ref[0] = zero[:WB]
    h2_ref[n2 + 1] = zero[:WB]
    step = iota((n1 * half, 256), 0) % half
    bias1, bias2 = rows_ref[0:1, :], rows_ref[1:2, :]
    for q in range(lanes // 256):
        cols = slice(q * 256, (q + 1) * 256)
        total = bias1
        for k in range(3):
            total = total + dot_nt(x_ref[k : k + n1].reshape(n1 * WB, 256), w1_ref[k, cols, :])
        total = jnp.maximum(total, 0.0)
        h1_ref[1 : n1 + 1, half : half + WB, cols] = total.reshape(n1, WB, 256).astype(BF16)
        parts = total.reshape(n1, 2, half, 256)
        even = parts[:, 0].reshape(n1 * half, 256)
        odd = parts[:, 1].reshape(n1 * half, 256)
        before = jnp.where(step == 0, 0.0, pltpu.roll(odd, 1, 0))
        after = jnp.where(step == half - 1, 0.0, pltpu.roll(even, n1 * half - 1, 0))
        h1_ref[1 : n1 + 1, 0:half, cols] = before.reshape(n1, half, 256).astype(BF16)
        h1_ref[1 : n1 + 1, half + WB :, cols] = after.reshape(n1, half, 256).astype(BF16)

    off2 = start2 - start1
    for q in range(lanes // 256):
        cols = slice(q * 256, (q + 1) * 256)
        lo, hi = max(q * 256 - 128, 0), min(q * 256 + 384, lanes)
        total = bias2
        for k in range(3):
            for l in range(3):
                cells_in = h1_ref[pl.ds(off2 + k, n2), l * half : l * half + WB, lo:hi].reshape(n2 * WB, hi - lo)
                total = total + dot_nt(cells_in, w2_ref[k * 3 + l, :, lo - q * 256 + 128 : hi - q * 256 + 128])
        h2_ref[1 : n2 + 1, :, cols] = jnp.maximum(total, 0.0).reshape(n2, WB, 256).astype(BF16)

    off3 = rows_here * trow - start2
    total = None
    for k in range(3):
        part = dot_nt(h2_ref[pl.ds(off3 + k, rows_here)].reshape(rows_here * WB, lanes), w3_ref[k])
        total = part if total is None else total + part
    for r in range(rows_here):
        for u in range(2):
            piece = total[(r * 2 + u) * half : (r * 2 + u + 1) * half]
            ya_ref[pl.ds(r * WB + u, half, stride=2), :] = piece[:, :128]
            yb_ref[pl.ds(r * WB + u, half, stride=2), :] = piece[:, 128:]
    here = rows_here * WB
    for v in range(here // 128):
        yt_ref[v, 0:128, :] = ya_ref[v * 128 : (v + 1) * 128, :].T
        yt_ref[v, 128:256, :] = yb_ref[v * 128 : (v + 1) * 128, :].T
    lane = iota((WA, here), 1)
    keep = (rows_here * trow + lane // WB).astype(F32) < count[:, :1]
    for ra in range(2):
        parts = [
            jnp.concatenate([yt_ref[v, pl.ds(l * 2 + ra, WA, stride=8), :] for v in range(here // 128)], axis=1)
            for l in range(3)
        ]
        before = jnp.where(lane % WB == 0, 0.0, pltpu.roll(parts[0], 1, 1))
        after = jnp.where(lane % WB == WB - 1, 0.0, pltpu.roll(parts[2], here - 1, 1))
        result = before + parts[1] + after + rows_ref[2:3, :1]
        out_ref[0, ra * WA : (ra + 1) * WA, :] = jnp.where(keep, result, 0.0)


def per_device(
    query_bank, ref_owner, target_feat, valid_rows, w_first, b_first, w_middle, b_middle, w_last, b_last
):
    target = target_feat[0]
    cells, width = target.shape
    positions = query_bank.shape[1]
    ch = w_middle.shape[0]
    group = 2 * ch
    lanes = WA * group
    trows = lax.axis_size("trow")
    grid_rows = cells // WB
    rows_here = grid_rows // trows
    sides = 1 if trows == 2 else 2
    n1, n2 = min(rows_here + 2 * sides, grid_rows), min(rows_here + sides, grid_rows)

    other = swapped(target, "trow", 1)
    own, sibling = spread(query_bank[0], ref_owner[0], "pair")
    ranks = jnp.stack([lax.axis_index("trow"), lax.axis_index("pair") % 2]).astype(jnp.int32)

    misc = jnp.concatenate([b_first, b_middle, b_last, valid_rows.astype(F32)])
    w1, w2, w3, rows = pl.pallas_call(
        functools.partial(expand_kernel, ch),
        out_shape=(
            jax.ShapeDtypeStruct((3, lanes, 256), BF16),
            jax.ShapeDtypeStruct((9, 256, 512), BF16),
            jax.ShapeDtypeStruct((3, 256, lanes), BF16),
            jax.ShapeDtypeStruct((8, 256), F32),
        ),
        in_specs=[VMEM] + [HBM] * 3,
        out_specs=(VMEM,) * 4,
        scratch_shapes=[
            pltpu.VMEM((27, 3, ch), BF16),
            pltpu.VMEM((81, ch, ch), BF16),
            pltpu.VMEM((27, 3, ch), BF16),
            pltpu.SemaphoreType.DMA((3,)),
        ],
        compiler_params=pltpu.CompilerParams(vmem_limit_bytes=VMEM_LIMIT),
        name="expand",
    )(
        jnp.broadcast_to(jnp.pad(misc, (0, 128 - misc.shape[0])), (8, 128)),
        in_hbm(jnp.transpose(w_first, (1, 2, 3, 4, 5, 0)).reshape(27, 3, ch)),
        in_hbm(jnp.transpose(w_middle, (2, 3, 4, 5, 0, 1)).reshape(81, ch, ch)),
        in_hbm(jnp.transpose(w_last, (0, 2, 3, 4, 5, 1)).reshape(27, 3, ch)),
    )

    return pl.pallas_call(
        functools.partial(score_kernel, rows_here, n1, n2),
        out_shape=jax.ShapeDtypeStruct((1, positions, rows_here * WB), F32),
        in_specs=[SMEM] + [VMEM] * 8,
        out_specs=VMEM,
        scratch_shapes=[
            pltpu.VMEM((8 + (grid_rows + 2) * PITCH, 128), F32),
            pltpu.VMEM((n1 + 2, WB, 256), BF16),
            pltpu.VMEM((n1 + 2, 2 * WB, lanes), BF16),
            pltpu.VMEM((n2 + 2, WB, lanes), BF16),
            pltpu.VMEM((rows_here * WB, 128), F32),
            pltpu.VMEM((rows_here * WB, 128), F32),
            pltpu.VMEM((rows_here * WB // 128, 256, 128), F32),
        ],
        compiler_params=pltpu.CompilerParams(vmem_limit_bytes=VMEM_LIMIT),
        name="score",
    )(ranks, rows, target, other, own, sibling, w1, w2, w3)


def solution(mesh):
    in_specs = (
        P("pair", None, None),
        P(),
        P("pair", None, "trow"),
        P("pair"),
        P(),
        P(),
        P(),
        P(),
        P(),
        P(),
    )
    out_specs = P("pair", None, "trow")
    return jax.shard_map(per_device, mesh=mesh, in_specs=in_specs, out_specs=out_specs, check_vma=False)
```

```python
import functools
import math

import jax
import jax.numpy as jnp
from jax import lax
from jax.experimental import pallas as pl
from jax.experimental.pallas import tpu as pltpu
from jax.sharding import PartitionSpec as P

WB = 32
WA = 32

EPS_NORM = 1e-06
EPS_PEAK = 1e-05

F32 = jnp.float32
BF16 = jnp.bfloat16
NT = (((1,), (1,)), ((), ()))
PITCH = WB + 8
VMEM_LIMIT = 16 * 1024 * 1024
VMEM = pl.BlockSpec(memory_space=pltpu.VMEM)
SMEM = pl.BlockSpec(memory_space=pltpu.SMEM)
HBM = pl.BlockSpec(memory_space=pltpu.HBM)


def swapped(values, axis, distance):
    count = lax.axis_size(axis)
    return lax.ppermute(values, axis, [(i, i ^ distance) for i in range(count)])


def front_kernel(axis, window_hbm, wf_hbm, wm_hbm, wl_hbm, mine_ref, wf_ref, wm_ref, wl_ref, sems):
    half = mine_ref.shape[0]
    rows = pl.ds(pl.multiple_of(lax.axis_index(axis) % 2 * half, half), half)
    pairs = ((window_hbm.at[rows], mine_ref), (wf_hbm, wf_ref), (wm_hbm, wm_ref), (wl_hbm, wl_ref))
    copies = [pltpu.make_async_copy(src, dst, sems.at[n]) for n, (src, dst) in enumerate(pairs)]
    for copy in copies:
        copy.start()
    for copy in copies:
        copy.wait()


def spread(window, owner, axis, target, weights, expand, rest):
    count = lax.axis_size(axis)
    rank = lax.axis_index(axis)
    half = window.shape[0] // 2
    theirs = swapped(window, axis, 1)
    mine, *weights = pl.pallas_call(
        functools.partial(front_kernel, axis),
        out_shape=[jax.ShapeDtypeStruct((half, window.shape[1]), window.dtype)]
        + [jax.ShapeDtypeStruct(w.shape, w.dtype) for w in weights],
        in_specs=[HBM] * 4,
        out_specs=[VMEM] * 4,
        scratch_shapes=[pltpu.SemaphoreType.DMA((4,))],
        compiler_params=pltpu.CompilerParams(vmem_limit_bytes=VMEM_LIMIT),
        name="front",
    )(in_hbm(window), *(in_hbm(w) for w in weights))
    expanded = expand(*weights)
    mine, target, owner = lax.optimization_barrier((mine, target, owner))
    other = swapped(target, "trow", 1)
    owner = owner[0]
    theirs = lax.dynamic_slice_in_dim(theirs, rank % 2 * half, half, 0)
    sibling = owner + 1 - 2 * (owner % 2)
    held = jnp.where(rank == owner, mine, jnp.where(rank == sibling, theirs, jnp.zeros_like(mine)))
    bits = [1 << b for b in range(1, count.bit_length() - 1)]
    rounds = [bits[at : at + 2] for at in range(0, len(bits), 2)]
    for n, near in enumerate(rounds):
        distances = near if len(near) == 1 else [sum(near), *near[::-1]]
        held = held + sum(swapped(held, axis, d) for d in distances)
        if n == 0:
            held, expanded, rest = lax.optimization_barrier((held, expanded, rest))
    b_last, valid_rows = rest
    rest = jnp.where(iota((8, 128), 0) == 0, b_last[0], valid_rows[0].astype(F32))
    held, rest = lax.optimization_barrier((held, rest))
    return held, swapped(held, axis, 1), other, expanded, rest


def in_hbm(array):
    return pltpu.with_memory_space_constraint(array, pltpu.HBM)


def dot(left, right):
    return jnp.dot(left, right, preferred_element_type=F32)


def dot_nt(left, right):
    return lax.dot_general(left, right, NT, preferred_element_type=F32)


def iota(shape, dim):
    return lax.broadcasted_iota(jnp.int32, shape, dim)


def one_hot(cond):
    return jnp.where(cond, 1.0, 0.0).astype(BF16)


def expand_kernel(
    ch, wf_ref, wm_ref, wl_ref, b1_hbm, b2_hbm, w1_ref, w2_ref, w3_ref, rows_ref, b1_ref, b2_ref, sems
):
    group = 2 * ch
    pairs = ((b1_hbm, b1_ref), (b2_hbm, b2_ref))
    copies = [pltpu.make_async_copy(src, dst, sems.at[n]) for n, (src, dst) in enumerate(pairs)]
    for copy in copies:
        copy.start()

    def by_offset(ref):
        values = ref[...].astype(F32)
        fill = jnp.zeros((32 - values.shape[0], ch), F32)
        return jnp.concatenate([part for l in range(3) for part in (values[:, l, :], fill)], axis=0)

    taps = by_offset(wf_ref)
    taps = jnp.concatenate([taps, jnp.zeros((32, ch), F32)], axis=0)
    taps = jnp.concatenate([taps, jnp.zeros((128, 128 - ch), F32)], axis=1).T[:ch].astype(BF16)
    lane = iota((128, 128), 1)
    src = iota((128, 128), 0)
    base = []
    for k in range(3):
        for ra in range(2):
            l, rp, j = lane // 6, (lane // 3) % 2, lane % 3
            want = l * 32 + ((rp - ra + 1) * 3 + j) * 3 + k
            base.append(dot(taps, one_hot((src == want) & (lane < 18))))
    base = jnp.concatenate(base, axis=0).astype(BF16)[:, :32]
    row = iota((32, 256), 0)
    col = iota((32, 256), 1)
    l, rp, j = row // 6, (row // 3) % 2, row % 3
    for ca in range(WA):
        at = ca + j - 1
        place = one_hot((col == l * 64 + rp * WA + at) & (at >= 0) & (at < WA) & (row < 18))
        block = dot(base, place).astype(BF16)
        for k in range(3):
            w1_ref[k, ca * group : (ca + 1) * group, :] = block[k * group : (k + 1) * group]

    total = None
    row = iota((ch, 128), 0)
    col = iota((ch, 128), 1)
    for j in range(3):
        for rp in range(2):
            picked = jnp.concatenate(
                [wm_ref[(((rp - ra + 1) * 3 + j) * 3 + k) * 3 + l] for k in range(3) for l in range(3) for ra in range(2)],
                axis=0,
            )
            part = dot(picked, one_hot(col == j * group + rp * ch + row))
            total = part if total is None else total + part
    base = total.astype(BF16)
    row = iota((128, 128), 0)
    col = iota((128, 128), 1)
    inner = [dot(base, one_hot((col == row + group * (ca - 1)) & (row < 3 * group))).astype(BF16) for ca in range(4)]
    outer = {
        (side, half): dot(
            base, one_hot((col == row + half * 64 + (-group if side else 0)) & (row // group == 2 * side))
        ).astype(BF16)
        for side in range(2)
        for half in range(2)
    }
    left = iota((group, 128), 1) < 64
    blank = jnp.zeros((group, 128), BF16)
    for k in range(3):
        tap = lambda values, l: values[(k * 3 + l) * group : (k * 3 + l + 1) * group] if 0 <= l < 3 else blank
        for u in range(2):
            for ca in range(4):
                rows = slice((u * 4 + ca) * group, (u * 4 + ca + 1) * group)
                for slab in range(4):
                    w2_ref[k, rows, slab * 128 : (slab + 1) * 128] = tap(inner[ca], slab - u)
                for v in range(2):
                    piece = blank
                    if ca in (0, 3):
                        side = ca // 3
                        piece = jnp.where(left, tap(outer[side, 0], 2 * v - u), tap(outer[side, 1], 2 * v + 1 - u))
                    w2_ref[k, rows, 512 + v * 128 : 640 + v * 128] = piece

    taps = by_offset(wl_ref).astype(BF16)
    out_row = iota((24, 96), 0)
    src = iota((24, 96), 1)
    row = iota((ch, 128), 0)
    col = iota((ch, 128), 1)
    total = None
    for j in range(3):
        for rp in range(2):
            k, l, ra = out_row // 8, (out_row % 8) // 2, out_row % 2
            want = l * 32 + ((rp - ra + 1) * 3 + j) * 3 + k
            picked = dot(one_hot((src == want) & (l < 3)), taps).astype(BF16)
            part = dot(picked, one_hot(col == j * group + rp * ch + row))
            total = part if total is None else total + part
    base = total.astype(BF16)
    row = iota((128, 256), 0)
    col = iota((128, 256), 1)
    moved = [dot(base, one_hot((col == row + group * b) & (row < 3 * group))) for b in range(4)]
    blank = jnp.zeros((8, 128), F32)
    lanes = WA * group // 128
    for k in range(3):
        for pair in range(WA // 2):
            for v in range(lanes):
                chunks = []
                for ca in (2 * pair, 2 * pair + 1):
                    a, b = (ca - 1) // 4, (ca - 1) % 4
                    piece = moved[b][k * 8 : (k + 1) * 8]
                    chunks.append(piece[:, :128] if v == a else piece[:, 128:] if v == a + 1 else blank)
                w3_ref[k, pair * 16 : (pair + 1) * 16, v * 128 : (v + 1) * 128] = jnp.concatenate(
                    chunks, axis=0
                ).astype(BF16)

    for copy in copies:
        copy.wait()

    chan = iota((1, 256), 1) % ch
    for n, ref in enumerate((b1_ref, b2_ref)):
        total = jnp.zeros((1, 256), F32)
        for o in range(ch):
            total = jnp.where(chan == o, ref[o], total)
        rows_ref[n : n + 1, :] = total


def score_kernel(
    rows_here, n1, n2, rest_ref, rows_ref, tm_ref, to_ref, qa_ref, qb_ref, w1_ref, w2_ref, w3_ref,
    out_ref, v_ref, x_ref, h1_ref, e_ref, h2_ref, ya_ref, yb_ref, yt_ref,
):
    trow, bit = lax.axis_index("trow"), lax.axis_index("pair") % 2
    count = rest_ref[1:2, :]
    cells = tm_ref.shape[0]
    grid_rows = cells // WB
    width = tm_ref.shape[1]
    scale = math.sqrt(2 * width)
    start1 = jnp.clip(rows_here * trow - 2, 0, grid_rows - n1)
    start2 = jnp.clip(rows_here * trow - 1, 0, grid_rows - n2)

    def unit(ref):
        values = ref[...].astype(F32)
        return (values * lax.rsqrt(jnp.sum(values * values, axis=1, keepdims=True) + EPS_NORM)).astype(BF16)

    qa, qb = unit(qa_ref), unit(qb_ref)
    own_first = bit == 0
    q0 = jnp.where(own_first, qa, qb)
    q1 = jnp.where(own_first, qb, qa)
    query = jnp.concatenate([q0, q1, q0, q1], axis=0)
    low, high = query[:, :width], query[:, width:]
    near = jnp.where(trow == 0, low, high)
    far = jnp.where(trow == 0, high, low)
    raw = dot_nt(tm_ref[...], near) + dot_nt(to_ref[...], far)

    def squares(ref):
        values = ref[...].astype(F32)
        return jnp.sum(values * values, axis=1, keepdims=True)

    inv = lax.rsqrt(squares(tm_ref) + squares(to_ref) + EPS_NORM)
    live = (iota((cells, 128), 0) // WB).astype(F32) < count
    corr = jnp.where(live, scale * raw * inv, 0.0)
    mag = jnp.abs(corr)
    peak_query = jnp.max(mag, axis=1, keepdims=True)
    peak_target = jnp.max(mag, axis=0, keepdims=True)
    volume = corr * (corr * (1.0 / (peak_query + EPS_PEAK))) * (corr * (1.0 / (peak_target + EPS_PEAK)))

    v_ref[0 : 8 + PITCH, :] = jnp.zeros((8 + PITCH, 128), F32)
    v_ref[8 + (grid_rows + 1) * PITCH :, :] = jnp.zeros((PITCH, 128), F32)
    for r in range(grid_rows):
        at = 8 + (r + 1) * PITCH
        v_ref[at : at + WB, :] = volume[r * WB : (r + 1) * WB]
        v_ref[at + WB : at + PITCH, :] = jnp.zeros((PITCH - WB, 128), F32)

    half = WB // 2
    left = iota((half, 128), 1) < 64
    for r in range(n1 + 2):
        at = pl.multiple_of((start1 + r) * PITCH, 8)
        slabs = [v_ref[pl.ds(at + 8 + o, half, stride=2), :] for o in (-1, 0, 1, 2)]
        for u in range(2):
            x_ref[r, u * half : (u + 1) * half, 0:128] = jnp.where(left, slabs[u], slabs[u + 1]).astype(BF16)
            x_ref[r, u * half : (u + 1) * half, 128:256] = jnp.where(left, slabs[u + 2], 0.0).astype(BF16)

    lanes = h1_ref.shape[2]
    zero = jnp.zeros((2 * WB, lanes), BF16)
    h1_ref[0] = zero
    h1_ref[n1 + 1] = zero
    h2_ref[0] = zero[:WB]
    h2_ref[n2 + 1] = zero[:WB]
    step = iota((n1 * half, 256), 0) % half
    bias1, bias2 = rows_ref[0:1, :], rows_ref[1:2, :]
    for q in range(lanes // 256):
        cols = slice(q * 256, (q + 1) * 256)
        total = bias1
        for k in range(3):
            total = total + dot_nt(x_ref[k : k + n1].reshape(n1 * WB, 256), w1_ref[k, cols, :])
        total = jnp.maximum(total, 0.0)
        h1_ref[1 : n1 + 1, half : half + WB, cols] = total.reshape(n1, WB, 256).astype(BF16)
        parts = total.reshape(n1, 2, half, 256)
        even = parts[:, 0].reshape(n1 * half, 256)
        odd = parts[:, 1].reshape(n1 * half, 256)
        before = jnp.where(step == 0, 0.0, pltpu.roll(odd, 1, 0))
        after = jnp.where(step == half - 1, 0.0, pltpu.roll(even, n1 * half - 1, 0))
        h1_ref[1 : n1 + 1, 0:half, cols] = before.reshape(n1, half, 256).astype(BF16)
        h1_ref[1 : n1 + 1, half + WB :, cols] = after.reshape(n1, half, 256).astype(BF16)

    lane = iota((n1, half, 128), 2)
    blank = jnp.zeros((n1, half, 128), BF16)
    blocks = lanes // 128
    e_ref[0] = jnp.zeros((half, 2 * lanes), BF16)
    e_ref[n1 + 1] = jnp.zeros((half, 2 * lanes), BF16)

    def turned(slab, block):
        if not 0 <= block < blocks:
            return blank
        values = h1_ref[1 : n1 + 1, slab * half : (slab + 1) * half, block * 128 : (block + 1) * 128]
        return pltpu.roll(values.reshape(n1 * half, 128), 96 if slab % 2 else 32, 1).reshape(n1, half, 128)

    for v in range(2):
        for q in range(blocks):
            one, two = 2 * v, 2 * v + 1
            first = jnp.where(lane < 32, turned(one, q - 1), turned(one, q + 1))
            second = jnp.where(lane < 96, turned(two, q - 1), turned(two, q + 1))
            e_ref[1 : n1 + 1, :, q * 256 + v * 128 : q * 256 + v * 128 + 128] = jnp.where(lane < 64, first, second)

    off2 = start2 - start1
    for q0 in range(0, blocks, 2):
        total = bias2
        for k in range(3):
            rows = pl.ds(off2 + k, n2)
            stack = []
            for q in range(q0, q0 + 2):
                parts = [h1_ref[rows, o * half : (o + 1) * half, q * 128 : (q + 1) * 128] for o in range(4)]
                parts.append(e_ref[rows, :, q * 256 : (q + 1) * 256])
                stack.append(jnp.concatenate([p.reshape(n2 * half, p.shape[2]) for p in parts], axis=1))
            total = total + dot_nt(jnp.concatenate(stack, axis=0), w2_ref[k])
        total = jnp.maximum(total, 0.0).reshape(2, n2, half, 256).astype(BF16)
        for q in range(q0, q0 + 2):
            for u in range(2):
                h2_ref[1 : n2 + 1, u * half : (u + 1) * half, q * 128 : (q + 1) * 128] = total[q - q0, :, :, u * 128 : (u + 1) * 128]

    off3 = rows_here * trow - start2
    total = None
    for k in range(3):
        part = dot_nt(h2_ref[pl.ds(off3 + k, rows_here)].reshape(rows_here * WB, lanes), w3_ref[k])
        total = part if total is None else total + part
    for r in range(rows_here):
        for u in range(2):
            piece = total[(r * 2 + u) * half : (r * 2 + u + 1) * half]
            ya_ref[pl.ds(r * WB + u, half, stride=2), :] = piece[:, :128]
            yb_ref[pl.ds(r * WB + u, half, stride=2), :] = piece[:, 128:]
    here = rows_here * WB
    for v in range(here // 128):
        yt_ref[v, 0:128, :] = ya_ref[v * 128 : (v + 1) * 128, :].T
        yt_ref[v, 128:256, :] = yb_ref[v * 128 : (v + 1) * 128, :].T
    lane = iota((WA, here), 1)
    keep = (rows_here * trow + lane // WB).astype(F32) < count[:, :1]
    for ra in range(2):
        parts = [
            jnp.concatenate([yt_ref[v, pl.ds(l * 2 + ra, WA, stride=8), :] for v in range(here // 128)], axis=1)
            for l in range(3)
        ]
        before = jnp.where(lane % WB == 0, 0.0, pltpu.roll(parts[0], 1, 1))
        after = jnp.where(lane % WB == WB - 1, 0.0, pltpu.roll(parts[2], here - 1, 1))
        result = before + parts[1] + after + rest_ref[0:1, :1]
        out_ref[0, ra * WA : (ra + 1) * WA, :] = jnp.where(keep, result, 0.0)


def per_device(
    query_bank, ref_owner, target_feat, valid_rows, w_first, b_first, w_middle, b_middle, w_last, b_last
):
    target = target_feat[0]
    cells, width = target.shape
    positions = query_bank.shape[1]
    ch = w_middle.shape[0]
    group = 2 * ch
    lanes = WA * group
    trows = lax.axis_size("trow")
    grid_rows = cells // WB
    rows_here = grid_rows // trows
    sides = 1 if trows == 2 else 2
    n1, n2 = min(rows_here + 2 * sides, grid_rows), min(rows_here + sides, grid_rows)

    expand = pl.pallas_call(
        functools.partial(expand_kernel, ch),
        out_shape=(
            jax.ShapeDtypeStruct((3, lanes, 256), BF16),
            jax.ShapeDtypeStruct((3, 256, 768), BF16),
            jax.ShapeDtypeStruct((3, 256, lanes), BF16),
            jax.ShapeDtypeStruct((8, 256), F32),
        ),
        in_specs=[VMEM] * 3 + [HBM] * 2,
        out_specs=(VMEM,) * 4,
        scratch_shapes=[
            pltpu.SMEM((ch,), F32),
            pltpu.SMEM((ch,), F32),
            pltpu.SemaphoreType.DMA((2,)),
        ],
        compiler_params=pltpu.CompilerParams(vmem_limit_bytes=VMEM_LIMIT),
        name="expand",
    )
    weights = (
        jnp.transpose(w_first, (1, 2, 3, 4, 5, 0)).reshape(27, 3, ch),
        jnp.transpose(w_middle, (2, 3, 4, 5, 0, 1)).reshape(81, ch, ch),
        jnp.transpose(w_last, (0, 2, 3, 4, 5, 1)).reshape(27, 3, ch),
    )
    biased = lambda *taps: expand(*taps, in_hbm(b_first), in_hbm(b_middle))
    own, sibling, other, (w1, w2, w3, rows), rest = spread(
        query_bank[0], ref_owner, "pair", target, weights, biased, (b_last, valid_rows)
    )
    return pl.pallas_call(
        functools.partial(score_kernel, rows_here, n1, n2),
        out_shape=jax.ShapeDtypeStruct((1, positions, rows_here * WB), F32),
        in_specs=[VMEM] * 9,
        out_specs=VMEM,
        scratch_shapes=[
            pltpu.VMEM((8 + (grid_rows + 2) * PITCH, 128), F32),
            pltpu.VMEM((n1 + 2, WB, 256), BF16),
            pltpu.VMEM((n1 + 2, 2 * WB, lanes), BF16),
            pltpu.VMEM((n1 + 2, WB // 2, 2 * lanes), BF16),
            pltpu.VMEM((n2 + 2, WB, lanes), BF16),
            pltpu.VMEM((rows_here * WB, 128), F32),
            pltpu.VMEM((rows_here * WB, 128), F32),
            pltpu.VMEM((rows_here * WB // 128, 256, 128), F32),
        ],
        compiler_params=pltpu.CompilerParams(vmem_limit_bytes=VMEM_LIMIT),
        name="score",
    )(rest, rows, target, other, own, sibling, w1, w2, w3)


def solution(mesh):
    in_specs = (
        P("pair", None, None),
        P(),
        P("pair", None, "trow"),
        P("pair"),
        P(),
        P(),
        P(),
        P(),
        P(),
        P(),
    )
    out_specs = P("pair", None, "trow")
    return jax.shard_map(per_device, mesh=mesh, in_specs=in_specs, out_specs=out_specs, check_vma=False)
```

```python
import functools
import math

import jax
import jax.numpy as jnp
from jax import lax
from jax.experimental import pallas as pl
from jax.experimental.pallas import tpu as pltpu
from jax.sharding import PartitionSpec as P

WB = 32
WA = 32

EPS_NORM = 1e-06
EPS_PEAK = 1e-05

F32 = jnp.float32
BF16 = jnp.bfloat16
NT = (((1,), (1,)), ((), ()))
PITCH = WB + 8
VMEM_LIMIT = 16 * 1024 * 1024
VMEM = pl.BlockSpec(memory_space=pltpu.VMEM)
SMEM = pl.BlockSpec(memory_space=pltpu.SMEM)
HBM = pl.BlockSpec(memory_space=pltpu.HBM)


def swapped(values, axis, distance):
    count = lax.axis_size(axis)
    return lax.ppermute(values, axis, [(i, i ^ distance) for i in range(count)])


def fetch_kernel(wf_hbm, wm_hbm, wl_hbm, wf_ref, wm_ref, wl_ref, sems):
    pairs = ((wf_hbm, wf_ref), (wm_hbm, wm_ref), (wl_hbm, wl_ref))
    copies = [pltpu.make_async_copy(src, dst, sems.at[n]) for n, (src, dst) in enumerate(pairs)]
    for copy in copies:
        copy.start()
    for copy in copies:
        copy.wait()


def front_kernel(axis, window_hbm, mine_ref, sem):
    half = mine_ref.shape[0]
    rows = pl.ds(pl.multiple_of(lax.axis_index(axis) % 2 * half, half), half)
    copy = pltpu.make_async_copy(window_hbm.at[rows], mine_ref, sem)
    copy.start()
    copy.wait()


def spread(window, owner, axis, target, weights, expand, rest):
    count = lax.axis_size(axis)
    rank = lax.axis_index(axis)
    half = window.shape[0] // 2
    theirs = swapped(window, axis, 1)
    fetch = pl.pallas_call(
        fetch_kernel,
        out_shape=[jax.ShapeDtypeStruct(w.shape, w.dtype) for w in weights],
        in_specs=[HBM] * 3,
        out_specs=[VMEM] * 3,
        scratch_shapes=[pltpu.SemaphoreType.DMA((3,))],
        compiler_params=pltpu.CompilerParams(vmem_limit_bytes=VMEM_LIMIT),
        name="fetch",
    )
    mine = pl.pallas_call(
        functools.partial(front_kernel, axis),
        out_shape=jax.ShapeDtypeStruct((half, window.shape[1]), window.dtype),
        in_specs=[HBM],
        out_specs=VMEM,
        scratch_shapes=[pltpu.SemaphoreType.DMA],
        compiler_params=pltpu.CompilerParams(vmem_limit_bytes=VMEM_LIMIT),
        name="front",
    )(in_hbm(window))
    mine, target, owner = lax.optimization_barrier((mine, target, owner))
    other = swapped(target, "trow", 1)
    owner = owner[0]
    theirs = lax.dynamic_slice_in_dim(theirs, rank % 2 * half, half, 0)
    sibling = owner + 1 - 2 * (owner % 2)
    held = jnp.where(rank == owner, mine, jnp.where(rank == sibling, theirs, jnp.zeros_like(mine)))
    held, weights = lax.optimization_barrier((held, weights))
    weights = fetch(*(in_hbm(w) for w in weights))
    bits = [1 << b for b in range(1, count.bit_length() - 1)]
    rounds = [bits[at : at + 2] for at in range(0, len(bits), 2)]
    for n, near in enumerate(rounds):
        distances = near if len(near) == 1 else [sum(near), *near[::-1]]
        held = held + sum(swapped(held, axis, d) for d in distances)
        if n == 0:
            held, weights, rest = lax.optimization_barrier((held, weights, rest))
            expanded = expand(*weights)
    b_last, valid_rows = rest
    rest = jnp.where(iota((8, 128), 0) == 0, b_last[0], valid_rows[0].astype(F32))
    held, rest, expanded = lax.optimization_barrier((held, rest, expanded))
    return held, swapped(held, axis, 1), other, expanded, rest


def in_hbm(array):
    return pltpu.with_memory_space_constraint(array, pltpu.HBM)


def dot(left, right):
    return jnp.dot(left, right, preferred_element_type=F32)


def dot_nt(left, right):
    return lax.dot_general(left, right, NT, preferred_element_type=F32)


def iota(shape, dim):
    return lax.broadcasted_iota(jnp.int32, shape, dim)


def one_hot(cond):
    return jnp.where(cond, 1.0, 0.0).astype(BF16)


def expand_kernel(
    ch, wf_ref, wm_ref, wl_ref, b1_hbm, b2_hbm, w1_ref, w2_ref, w3_ref, rows_ref, b1_ref, b2_ref, sems
):
    group = 2 * ch
    pairs = ((b1_hbm, b1_ref), (b2_hbm, b2_ref))
    copies = [pltpu.make_async_copy(src, dst, sems.at[n]) for n, (src, dst) in enumerate(pairs)]
    for copy in copies:
        copy.start()

    def by_offset(ref):
        values = ref[...].astype(F32)
        fill = jnp.zeros((32 - values.shape[0], ch), F32)
        return jnp.concatenate([part for l in range(3) for part in (values[:, l, :], fill)], axis=0)

    taps = by_offset(wf_ref)
    taps = jnp.concatenate([taps, jnp.zeros((32, ch), F32)], axis=0)
    taps = jnp.concatenate([taps, jnp.zeros((128, 128 - ch), F32)], axis=1).T[:ch].astype(BF16)
    lane = iota((128, 128), 1)
    src = iota((128, 128), 0)
    base = []
    for k in range(3):
        for ra in range(2):
            l, rp, j = lane // 6, (lane // 3) % 2, lane % 3
            want = l * 32 + ((rp - ra + 1) * 3 + j) * 3 + k
            base.append(dot(taps, one_hot((src == want) & (lane < 18))))
    base = jnp.concatenate(base, axis=0).astype(BF16)[:, :32]
    row = iota((32, 256), 0)
    col = iota((32, 256), 1)
    l, rp, j = row // 6, (row // 3) % 2, row % 3
    for ca in range(WA):
        at = ca + j - 1
        place = one_hot((col == l * 64 + rp * WA + at) & (at >= 0) & (at < WA) & (row < 18))
        block = dot(base, place).astype(BF16)
        for k in range(3):
            w1_ref[k, ca * group : (ca + 1) * group, :] = block[k * group : (k + 1) * group]

    total = None
    row = iota((ch, 128), 0)
    col = iota((ch, 128), 1)
    for j in range(3):
        for rp in range(2):
            picked = jnp.concatenate(
                [wm_ref[(((rp - ra + 1) * 3 + j) * 3 + k) * 3 + l] for k in range(3) for l in range(3) for ra in range(2)],
                axis=0,
            )
            part = dot(picked, one_hot(col == j * group + rp * ch + row))
            total = part if total is None else total + part
    base = total.astype(BF16)
    row = iota((128, 128), 0)
    col = iota((128, 128), 1)
    inner = [dot(base, one_hot((col == row + group * (ca - 1)) & (row < 3 * group))).astype(BF16) for ca in range(4)]
    outer = {
        (side, half): dot(
            base, one_hot((col == row + half * 64 + (-group if side else 0)) & (row // group == 2 * side))
        ).astype(BF16)
        for side in range(2)
        for half in range(2)
    }
    left = iota((group, 128), 1) < 64
    blank = jnp.zeros((group, 128), BF16)
    for k in range(3):
        tap = lambda values, l: values[(k * 3 + l) * group : (k * 3 + l + 1) * group] if 0 <= l < 3 else blank
        for u in range(2):
            for ca in range(4):
                rows = slice((u * 4 + ca) * group, (u * 4 + ca + 1) * group)
                for slab in range(4):
                    w2_ref[k, rows, slab * 128 : (slab + 1) * 128] = tap(inner[ca], slab - u)
                for v in range(2):
                    piece = blank
                    if ca in (0, 3):
                        side = ca // 3
                        piece = jnp.where(left, tap(outer[side, 0], 2 * v - u), tap(outer[side, 1], 2 * v + 1 - u))
                    w2_ref[k, rows, 512 + v * 128 : 640 + v * 128] = piece

    taps = by_offset(wl_ref).astype(BF16)
    out_row = iota((24, 96), 0)
    src = iota((24, 96), 1)
    row = iota((ch, 128), 0)
    col = iota((ch, 128), 1)
    total = None
    for j in range(3):
        for rp in range(2):
            k, l, ra = out_row // 8, (out_row % 8) // 2, out_row % 2
            want = l * 32 + ((rp - ra + 1) * 3 + j) * 3 + k
            picked = dot(one_hot((src == want) & (l < 3)), taps).astype(BF16)
            part = dot(picked, one_hot(col == j * group + rp * ch + row))
            total = part if total is None else total + part
    base = total.astype(BF16)
    row = iota((128, 256), 0)
    col = iota((128, 256), 1)
    moved = [dot(base, one_hot((col == row + group * b) & (row < 3 * group))) for b in range(4)]
    blank = jnp.zeros((8, 128), F32)
    lanes = WA * group // 128
    for k in range(3):
        for pair in range(WA // 2):
            for v in range(lanes):
                chunks = []
                for ca in (2 * pair, 2 * pair + 1):
                    a, b = (ca - 1) // 4, (ca - 1) % 4
                    piece = moved[b][k * 8 : (k + 1) * 8]
                    chunks.append(piece[:, :128] if v == a else piece[:, 128:] if v == a + 1 else blank)
                w3_ref[k, pair * 16 : (pair + 1) * 16, v * 128 : (v + 1) * 128] = jnp.concatenate(
                    chunks, axis=0
                ).astype(BF16)

    for copy in copies:
        copy.wait()

    chan = iota((1, 256), 1) % ch
    for n, ref in enumerate((b1_ref, b2_ref)):
        total = jnp.zeros((1, 256), F32)
        for o in range(ch):
            total = jnp.where(chan == o, ref[o], total)
        rows_ref[n : n + 1, :] = total


def score_kernel(
    rows_here, n1, n2, rest_ref, rows_ref, tm_ref, to_ref, qa_ref, qb_ref, w1_ref, w2_ref, w3_ref,
    out_ref, v_ref, x_ref, ya_ref, yb_ref, yt_ref, *layers,
):
    trow, bit = lax.axis_index("trow"), lax.axis_index("pair") % 2
    count = rest_ref[1:2, :]
    cells = tm_ref.shape[0]
    grid_rows = cells // WB
    width = tm_ref.shape[1]
    scale = math.sqrt(2 * width)
    start1 = jnp.clip(rows_here * trow - 2, 0, grid_rows - n1)
    start2 = jnp.clip(rows_here * trow - 1, 0, grid_rows - n2)

    def unit(ref):
        values = ref[...].astype(F32)
        return (values * lax.rsqrt(jnp.sum(values * values, axis=1, keepdims=True) + EPS_NORM)).astype(BF16)

    qa, qb = unit(qa_ref), unit(qb_ref)
    own_first = bit == 0
    q0 = jnp.where(own_first, qa, qb)
    q1 = jnp.where(own_first, qb, qa)
    query = jnp.concatenate([q0, q1, q0, q1], axis=0)
    low, high = query[:, :width], query[:, width:]
    near = jnp.where(trow == 0, low, high)
    far = jnp.where(trow == 0, high, low)
    raw = dot_nt(tm_ref[...], near) + dot_nt(to_ref[...], far)

    def squares(ref):
        values = ref[...].astype(F32)
        return jnp.sum(values * values, axis=1, keepdims=True)

    inv = lax.rsqrt(squares(tm_ref) + squares(to_ref) + EPS_NORM)
    live = (iota((cells, 128), 0) // WB).astype(F32) < count
    corr = jnp.where(live, scale * raw * inv, 0.0)
    mag = jnp.abs(corr)
    peak_query = jnp.max(mag, axis=1, keepdims=True)
    peak_target = jnp.max(mag, axis=0, keepdims=True)
    volume = corr * (corr * (1.0 / (peak_query + EPS_PEAK))) * (corr * (1.0 / (peak_target + EPS_PEAK)))

    v_ref[0 : 8 + PITCH, :] = jnp.zeros((8 + PITCH, 128), F32)
    v_ref[8 + (grid_rows + 1) * PITCH :, :] = jnp.zeros((PITCH, 128), F32)
    for r in range(grid_rows):
        at = 8 + (r + 1) * PITCH
        v_ref[at : at + WB, :] = volume[r * WB : (r + 1) * WB]
        v_ref[at + WB : at + PITCH, :] = jnp.zeros((PITCH - WB, 128), F32)

    half = WB // 2
    left = iota((half, 128), 1) < 64
    for r in range(n1 + 2):
        at = pl.multiple_of((start1 + r) * PITCH, 8)
        slabs = [v_ref[pl.ds(at + 8 + o, half, stride=2), :] for o in (-1, 0, 1, 2)]
        for u in range(2):
            x_ref[r, u * half : (u + 1) * half, 0:128] = jnp.where(left, slabs[u], slabs[u + 1]).astype(BF16)
            x_ref[r, u * half : (u + 1) * half, 128:256] = jnp.where(left, slabs[u + 2], 0.0).astype(BF16)

    groups = len(layers) // 3
    h1_refs, e_refs, h2_refs = layers[:groups], layers[groups : 2 * groups], layers[2 * groups :]
    for ref, count1 in [(r, n1) for r in (*h1_refs, *e_refs)] + [(r, n2) for r in h2_refs]:
        ref[0] = jnp.zeros(ref.shape[1:], BF16)
        ref[count1 + 1] = jnp.zeros(ref.shape[1:], BF16)
    bias1, bias2 = rows_ref[0:1, :], rows_ref[1:2, :]
    off2 = start2 - start1
    off3 = rows_here * trow - start2
    step = iota((n1 * half, 256), 0) % half

    def first_layer(g):
        cols = slice(g * 256, (g + 1) * 256)
        total = bias1
        for k in range(3):
            total = total + dot_nt(x_ref[k : k + n1].reshape(n1 * WB, 256), w1_ref[k, cols, :])
        total = jnp.maximum(total, 0.0)
        ref = h1_refs[g]
        ref[1 : n1 + 1, half : half + WB, :] = total.reshape(n1, WB, 256).astype(BF16)
        parts = total.reshape(n1, 2, half, 256)
        even = parts[:, 0].reshape(n1 * half, 256)
        odd = parts[:, 1].reshape(n1 * half, 256)
        before = jnp.where(step == 0, 0.0, pltpu.roll(odd, 1, 0))
        after = jnp.where(step == half - 1, 0.0, pltpu.roll(even, n1 * half - 1, 0))
        ref[1 : n1 + 1, 0:half, :] = before.reshape(n1, half, 256).astype(BF16)
        ref[1 : n1 + 1, half + WB :, :] = after.reshape(n1, half, 256).astype(BF16)

    lane = iota((n1, half, 128), 2)
    blank = jnp.zeros((n1, half, 128), BF16)

    def turned(slab, block):
        if not 0 <= block < 2 * groups:
            return blank
        g, part = divmod(block, 2)
        values = h1_refs[g][1 : n1 + 1, slab * half : (slab + 1) * half, part * 128 : (part + 1) * 128]
        return pltpu.roll(values.reshape(n1 * half, 128), 96 if slab % 2 else 32, 1).reshape(n1, half, 128)

    def borders(g):
        for part in range(2):
            block = 2 * g + part
            for v in range(2):
                one, two = 2 * v, 2 * v + 1
                first = jnp.where(lane < 32, turned(one, block - 1), turned(one, block + 1))
                second = jnp.where(lane < 96, turned(two, block - 1), turned(two, block + 1))
                at = part * 256 + v * 128
                e_refs[g][1 : n1 + 1, :, at : at + 128] = jnp.where(lane < 64, first, second)

    def middle_layer(g):
        total = bias2
        for k in range(3):
            rows = pl.ds(off2 + k, n2)
            stack = []
            for part in range(2):
                parts = [
                    h1_refs[g][rows, o * half : (o + 1) * half, part * 128 : (part + 1) * 128] for o in range(4)
                ]
                parts.append(e_refs[g][rows, :, part * 256 : (part + 1) * 256])
                stack.append(jnp.concatenate([p.reshape(n2 * half, p.shape[2]) for p in parts], axis=1))
            total = total + dot_nt(jnp.concatenate(stack, axis=0), w2_ref[k])
        total = jnp.maximum(total, 0.0).reshape(2, n2, half, 256).astype(BF16)
        for part in range(2):
            for u in range(2):
                h2_refs[g][1 : n2 + 1, u * half : (u + 1) * half, part * 128 : (part + 1) * 128] = total[
                    part, :, :, u * 128 : (u + 1) * 128
                ]

    def last_layer(g):
        parts = []
        for k in range(3):
            cells_in = h2_refs[g][pl.ds(off3 + k, rows_here)].reshape(rows_here * WB, 256)
            parts.append(dot_nt(cells_in, w3_ref[k, :, g * 256 : (g + 1) * 256]))
        return sum(parts)

    for g in range(groups):
        first_layer(g)
    for g in range(groups):
        borders(g)
    for g in range(groups):
        middle_layer(g)
    total = sum(last_layer(g) for g in range(groups))
    for r in range(rows_here):
        for u in range(2):
            piece = total[(r * 2 + u) * half : (r * 2 + u + 1) * half]
            ya_ref[pl.ds(r * WB + u, half, stride=2), :] = piece[:, :128]
            yb_ref[pl.ds(r * WB + u, half, stride=2), :] = piece[:, 128:]
    here = rows_here * WB
    for v in range(here // 128):
        yt_ref[v, 0:128, :] = ya_ref[v * 128 : (v + 1) * 128, :].T
        yt_ref[v, 128:256, :] = yb_ref[v * 128 : (v + 1) * 128, :].T
    lane = iota((WA, here), 1)
    keep = (rows_here * trow + lane // WB).astype(F32) < count[:, :1]
    for ra in range(2):
        parts = [
            jnp.concatenate([yt_ref[v, pl.ds(l * 2 + ra, WA, stride=8), :] for v in range(here // 128)], axis=1)
            for l in range(3)
        ]
        before = jnp.where(lane % WB == 0, 0.0, pltpu.roll(parts[0], 1, 1))
        after = jnp.where(lane % WB == WB - 1, 0.0, pltpu.roll(parts[2], here - 1, 1))
        result = before + parts[1] + after + rest_ref[0:1, :1]
        out_ref[0, ra * WA : (ra + 1) * WA, :] = jnp.where(keep, result, 0.0)


def per_device(
    query_bank, ref_owner, target_feat, valid_rows, w_first, b_first, w_middle, b_middle, w_last, b_last
):
    target = target_feat[0]
    cells, width = target.shape
    positions = query_bank.shape[1]
    ch = w_middle.shape[0]
    group = 2 * ch
    lanes = WA * group
    trows = lax.axis_size("trow")
    grid_rows = cells // WB
    rows_here = grid_rows // trows
    sides = 1 if trows == 2 else 2
    n1, n2 = min(rows_here + 2 * sides, grid_rows), min(rows_here + sides, grid_rows)

    expand = pl.pallas_call(
        functools.partial(expand_kernel, ch),
        out_shape=(
            jax.ShapeDtypeStruct((3, lanes, 256), BF16),
            jax.ShapeDtypeStruct((3, 256, 768), BF16),
            jax.ShapeDtypeStruct((3, 256, lanes), BF16),
            jax.ShapeDtypeStruct((8, 256), F32),
        ),
        in_specs=[VMEM] * 3 + [HBM] * 2,
        out_specs=(VMEM,) * 4,
        scratch_shapes=[
            pltpu.SMEM((ch,), F32),
            pltpu.SMEM((ch,), F32),
            pltpu.SemaphoreType.DMA((2,)),
        ],
        compiler_params=pltpu.CompilerParams(vmem_limit_bytes=VMEM_LIMIT),
        name="expand",
    )
    weights = (
        jnp.transpose(w_first, (1, 2, 3, 4, 5, 0)).reshape(27, 3, ch),
        jnp.transpose(w_middle, (2, 3, 4, 5, 0, 1)).reshape(81, ch, ch),
        jnp.transpose(w_last, (0, 2, 3, 4, 5, 1)).reshape(27, 3, ch),
    )
    biased = lambda *taps: expand(*taps, in_hbm(b_first), in_hbm(b_middle))
    own, sibling, other, (w1, w2, w3, rows), rest = spread(
        query_bank[0], ref_owner, "pair", target, weights, biased, (b_last, valid_rows)
    )
    return pl.pallas_call(
        functools.partial(score_kernel, rows_here, n1, n2),
        out_shape=jax.ShapeDtypeStruct((1, positions, rows_here * WB), F32),
        in_specs=[VMEM] * 9,
        out_specs=VMEM,
        scratch_shapes=[
            pltpu.VMEM((8 + (grid_rows + 2) * PITCH, 128), F32),
            pltpu.VMEM((n1 + 2, WB, 256), BF16),
            pltpu.VMEM((rows_here * WB, 128), F32),
            pltpu.VMEM((rows_here * WB, 128), F32),
            pltpu.VMEM((rows_here * WB // 128, 256, 128), F32),
            *[pltpu.VMEM((n1 + 2, 2 * WB, 256), BF16)] * (lanes // 256),
            *[pltpu.VMEM((n1 + 2, WB // 2, 512), BF16)] * (lanes // 256),
            *[pltpu.VMEM((n2 + 2, WB, 256), BF16)] * (lanes // 256),
        ],
        compiler_params=pltpu.CompilerParams(vmem_limit_bytes=VMEM_LIMIT),
        name="score",
    )(rest, rows, target, other, own, sibling, w1, w2, w3)


def solution(mesh):
    in_specs = (
        P("pair", None, None),
        P(),
        P("pair", None, "trow"),
        P("pair"),
        P(),
        P(),
        P(),
        P(),
        P(),
        P(),
    )
    out_specs = P("pair", None, "trow")
    return jax.shard_map(per_device, mesh=mesh, in_specs=in_specs, out_specs=out_specs, check_vma=False)
```

```python
import functools
import math

import jax
import jax.numpy as jnp
from jax import lax
from jax.experimental import pallas as pl
from jax.experimental.pallas import tpu as pltpu
from jax.sharding import PartitionSpec as P

WB = 32
WA = 32

EPS_NORM = 1e-06
EPS_PEAK = 1e-05

F32 = jnp.float32
BF16 = jnp.bfloat16
NT = (((1,), (1,)), ((), ()))
PITCH = WB + 8
VMEM_LIMIT = 16 * 1024 * 1024
VMEM = pl.BlockSpec(memory_space=pltpu.VMEM)
SMEM = pl.BlockSpec(memory_space=pltpu.SMEM)
HBM = pl.BlockSpec(memory_space=pltpu.HBM)


def swapped(values, axis, distance):
    count = lax.axis_size(axis)
    return lax.ppermute(values, axis, [(i, i ^ distance) for i in range(count)])


def fetch_kernel(wf_hbm, wm_hbm, wl_hbm, wf_ref, wm_ref, wl_ref, sems):
    pairs = ((wf_hbm, wf_ref), (wm_hbm, wm_ref), (wl_hbm, wl_ref))
    copies = [pltpu.make_async_copy(src, dst, sems.at[n]) for n, (src, dst) in enumerate(pairs)]
    for copy in copies:
        copy.start()
    for copy in copies:
        copy.wait()


def front_kernel(axis, window_hbm, mine_ref, sem):
    half = mine_ref.shape[0]
    rows = pl.ds(pl.multiple_of(lax.axis_index(axis) % 2 * half, half), half)
    copy = pltpu.make_async_copy(window_hbm.at[rows], mine_ref, sem)
    copy.start()
    copy.wait()


def spread(window, owner, axis, target, weights, expand, rest):
    count = lax.axis_size(axis)
    rank = lax.axis_index(axis)
    half = window.shape[0] // 2
    theirs = swapped(window, axis, 1)
    fetch = pl.pallas_call(
        fetch_kernel,
        out_shape=[jax.ShapeDtypeStruct(w.shape, w.dtype) for w in weights],
        in_specs=[HBM] * 3,
        out_specs=[VMEM] * 3,
        scratch_shapes=[pltpu.SemaphoreType.DMA((3,))],
        compiler_params=pltpu.CompilerParams(vmem_limit_bytes=VMEM_LIMIT),
        name="fetch",
    )
    mine = pl.pallas_call(
        functools.partial(front_kernel, axis),
        out_shape=jax.ShapeDtypeStruct((half, window.shape[1]), window.dtype),
        in_specs=[HBM],
        out_specs=VMEM,
        scratch_shapes=[pltpu.SemaphoreType.DMA],
        compiler_params=pltpu.CompilerParams(vmem_limit_bytes=VMEM_LIMIT),
        name="front",
    )(in_hbm(window))
    mine, target, owner = lax.optimization_barrier((mine, target, owner))
    other = swapped(target, "trow", 1)
    owner = owner[0]
    theirs = lax.dynamic_slice_in_dim(theirs, rank % 2 * half, half, 0)
    sibling = owner + 1 - 2 * (owner % 2)
    held = jnp.where(rank == owner, mine, jnp.where(rank == sibling, theirs, jnp.zeros_like(mine)))
    held, weights = lax.optimization_barrier((held, weights))
    weights = fetch(*(in_hbm(w) for w in weights))
    bits = [1 << b for b in range(1, count.bit_length() - 1)]
    rounds = [bits[at : at + 2] for at in range(0, len(bits), 2)]
    for n, near in enumerate(rounds):
        distances = near if len(near) == 1 else [sum(near), *near[::-1]]
        held = held + sum(swapped(held, axis, d) for d in distances)
        if n == 0:
            held, weights, rest = lax.optimization_barrier((held, weights, rest))
            expanded = expand(*weights)
    b_last, valid_rows = rest
    rest = jnp.where(iota((8, 128), 0) == 0, b_last[0], valid_rows[0].astype(F32))
    held, rest, expanded = lax.optimization_barrier((held, rest, expanded))
    return held, swapped(held, axis, 1), other, expanded, rest


def in_hbm(array):
    return pltpu.with_memory_space_constraint(array, pltpu.HBM)


def dot(left, right):
    return jnp.dot(left, right, preferred_element_type=F32)


def dot_nt(left, right):
    return lax.dot_general(left, right, NT, preferred_element_type=F32)


def iota(shape, dim):
    return lax.broadcasted_iota(jnp.int32, shape, dim)


def one_hot(cond):
    return jnp.where(cond, 1.0, 0.0).astype(BF16)


def expand_kernel(
    ch, wf_ref, wm_ref, wl_ref, b1_hbm, b2_hbm, w1_ref, w2_ref, w3_ref, rows_ref, b1_ref, b2_ref, sems
):
    group = 2 * ch
    pairs = ((b1_hbm, b1_ref), (b2_hbm, b2_ref))
    copies = [pltpu.make_async_copy(src, dst, sems.at[n]) for n, (src, dst) in enumerate(pairs)]
    for copy in copies:
        copy.start()

    def by_offset(ref):
        values = ref[...].astype(F32)
        fill = jnp.zeros((32 - values.shape[0], ch), F32)
        return jnp.concatenate([part for l in range(3) for part in (values[:, l, :], fill)], axis=0)

    taps = by_offset(wf_ref)
    taps = jnp.concatenate([taps, jnp.zeros((32, ch), F32)], axis=0)
    taps = jnp.concatenate([taps, jnp.zeros((128, 128 - ch), F32)], axis=1).T[:ch].astype(BF16)
    lane = iota((128, 128), 1)
    src = iota((128, 128), 0)
    base = []
    for k in range(3):
        for ra in range(2):
            l, rp, j = lane // 6, (lane // 3) % 2, lane % 3
            want = l * 32 + ((rp - ra + 1) * 3 + j) * 3 + k
            base.append(dot(taps, one_hot((src == want) & (lane < 18))))
    base = jnp.concatenate(base, axis=0).astype(BF16)[:, :32]
    row = iota((32, 256), 0)
    col = iota((32, 256), 1)
    l, rp, j = row // 6, (row // 3) % 2, row % 3
    for ca in range(WA):
        at = ca + j - 1
        place = one_hot((col == l * 64 + rp * WA + at) & (at >= 0) & (at < WA) & (row < 18))
        block = dot(base, place).astype(BF16)
        for k in range(3):
            w1_ref[k, ca * group : (ca + 1) * group, :] = block[k * group : (k + 1) * group]

    total = None
    row = iota((ch, 128), 0)
    col = iota((ch, 128), 1)
    for j in range(3):
        for rp in range(2):
            picked = jnp.concatenate(
                [wm_ref[(((rp - ra + 1) * 3 + j) * 3 + k) * 3 + l] for k in range(3) for l in range(3) for ra in range(2)],
                axis=0,
            )
            part = dot(picked, one_hot(col == j * group + rp * ch + row))
            total = part if total is None else total + part
    base = total.astype(BF16)
    row = iota((128, 128), 0)
    col = iota((128, 128), 1)
    inner = [dot(base, one_hot((col == row + group * (ca - 1)) & (row < 3 * group))).astype(BF16) for ca in range(4)]
    outer = {
        (side, half): dot(
            base, one_hot((col == row + half * 64 + (-group if side else 0)) & (row // group == 2 * side))
        ).astype(BF16)
        for side in range(2)
        for half in range(2)
    }
    left = iota((group, 128), 1) < 64
    blank = jnp.zeros((group, 128), BF16)
    for k in range(3):
        tap = lambda values, l: values[(k * 3 + l) * group : (k * 3 + l + 1) * group] if 0 <= l < 3 else blank
        for u in range(2):
            for ca in range(4):
                rows = slice((u * 4 + ca) * group, (u * 4 + ca + 1) * group)
                for slab in range(4):
                    w2_ref[k, rows, slab * 128 : (slab + 1) * 128] = tap(inner[ca], slab - u)
                for v in range(2):
                    piece = blank
                    if ca in (0, 3):
                        side = ca // 3
                        piece = jnp.where(left, tap(outer[side, 0], 2 * v - u), tap(outer[side, 1], 2 * v + 1 - u))
                    w2_ref[k, rows, 512 + v * 128 : 640 + v * 128] = piece

    taps = by_offset(wl_ref).astype(BF16)
    out_row = iota((24, 96), 0)
    src = iota((24, 96), 1)
    row = iota((ch, 128), 0)
    col = iota((ch, 128), 1)
    total = None
    for j in range(3):
        for rp in range(2):
            k, l, ra = out_row // 8, (out_row % 8) // 2, out_row % 2
            want = l * 32 + ((rp - ra + 1) * 3 + j) * 3 + k
            picked = dot(one_hot((src == want) & (l < 3)), taps).astype(BF16)
            part = dot(picked, one_hot(col == j * group + rp * ch + row))
            total = part if total is None else total + part
    base = total.astype(BF16)
    row = iota((128, 256), 0)
    col = iota((128, 256), 1)
    moved = [dot(base, one_hot((col == row + group * b) & (row < 3 * group))) for b in range(4)]
    blank = jnp.zeros((8, 128), F32)
    lanes = WA * group // 128
    for k in range(3):
        for pair in range(WA // 2):
            for v in range(lanes):
                chunks = []
                for ca in (2 * pair, 2 * pair + 1):
                    a, b = (ca - 1) // 4, (ca - 1) % 4
                    piece = moved[b][k * 8 : (k + 1) * 8]
                    chunks.append(piece[:, :128] if v == a else piece[:, 128:] if v == a + 1 else blank)
                w3_ref[k, pair * 16 : (pair + 1) * 16, v * 128 : (v + 1) * 128] = jnp.concatenate(
                    chunks, axis=0
                ).astype(BF16)

    for copy in copies:
        copy.wait()

    chan = iota((1, 256), 1) % ch
    for n, ref in enumerate((b1_ref, b2_ref)):
        total = jnp.zeros((1, 256), F32)
        for o in range(ch):
            total = jnp.where(chan == o, ref[o], total)
        rows_ref[n : n + 1, :] = total


def score_kernel(
    rows_here, n1, n2, rest_ref, rows_ref, tm_ref, to_ref, qa_ref, qb_ref, w1_ref, w2_ref, w3_ref,
    out_ref, v_ref, x_ref, ya_ref, yb_ref, yt_ref, *layers,
):
    trow, bit = lax.axis_index("trow"), lax.axis_index("pair") % 2
    count = rest_ref[1:2, :]
    cells = tm_ref.shape[0]
    grid_rows = cells // WB
    width = tm_ref.shape[1]
    scale = math.sqrt(2 * width)
    start1 = jnp.clip(rows_here * trow - 2, 0, grid_rows - n1)
    start2 = jnp.clip(rows_here * trow - 1, 0, grid_rows - n2)

    def unit(ref):
        values = ref[...].astype(F32)
        return (values * lax.rsqrt(jnp.sum(values * values, axis=1, keepdims=True) + EPS_NORM)).astype(BF16)

    qa, qb = unit(qa_ref), unit(qb_ref)
    own_first = bit == 0
    q0 = jnp.where(own_first, qa, qb)
    q1 = jnp.where(own_first, qb, qa)
    query = jnp.concatenate([q0, q1, q0, q1], axis=0)
    low, high = query[:, :width], query[:, width:]
    near = jnp.where(trow == 0, low, high)
    far = jnp.where(trow == 0, high, low)
    raw = dot_nt(tm_ref[...], near) + dot_nt(to_ref[...], far)

    def squares(ref):
        values = ref[...].astype(F32)
        return jnp.sum(values * values, axis=1, keepdims=True)

    inv = lax.rsqrt(squares(tm_ref) + squares(to_ref) + EPS_NORM)
    live = (iota((cells, 128), 0) // WB).astype(F32) < count
    corr = jnp.where(live, scale * raw * inv, 0.0)
    mag = jnp.abs(corr)
    peak_query = jnp.max(mag, axis=1, keepdims=True)
    peak_target = jnp.max(mag, axis=0, keepdims=True)
    volume = corr * (corr * (1.0 / (peak_query + EPS_PEAK))) * (corr * (1.0 / (peak_target + EPS_PEAK)))

    v_ref[0 : 8 + PITCH, :] = jnp.zeros((8 + PITCH, 128), F32)
    v_ref[8 + (grid_rows + 1) * PITCH :, :] = jnp.zeros((PITCH, 128), F32)
    for r in range(grid_rows):
        at = 8 + (r + 1) * PITCH
        v_ref[at : at + WB, :] = volume[r * WB : (r + 1) * WB]
        v_ref[at + WB : at + PITCH, :] = jnp.zeros((PITCH - WB, 128), F32)

    half = WB // 2
    left = iota((half, 128), 1) < 64
    for r in range(n1 + 2):
        at = pl.multiple_of((start1 + r) * PITCH, 8)
        slabs = [v_ref[pl.ds(at + 8 + o, half, stride=2), :] for o in (-1, 0, 1, 2)]
        for u in range(2):
            x_ref[r, u * half : (u + 1) * half, 0:128] = jnp.where(left, slabs[u], slabs[u + 1]).astype(BF16)
            x_ref[r, u * half : (u + 1) * half, 128:256] = jnp.where(left, slabs[u + 2], 0.0).astype(BF16)

    groups = len(layers) // 3
    h1_refs, e_refs, h2_refs = layers[:groups], layers[groups : 2 * groups], layers[2 * groups :]
    for ref, count1 in [(r, n1) for r in (*h1_refs, *e_refs)] + [(r, n2) for r in h2_refs]:
        ref[0] = jnp.zeros(ref.shape[1:], BF16)
        ref[count1 + 1] = jnp.zeros(ref.shape[1:], BF16)
    bias1, bias2 = rows_ref[0:1, :], rows_ref[1:2, :]
    off2 = start2 - start1
    off3 = rows_here * trow - start2
    step = iota((n1 * half, 256), 0) % half

    def first_layer(g):
        cols = slice(g * 256, (g + 1) * 256)
        total = bias1
        for k in range(3):
            total = total + dot_nt(x_ref[k : k + n1].reshape(n1 * WB, 256), w1_ref[k, cols, :])
        total = jnp.maximum(total, 0.0)
        ref = h1_refs[g]
        ref[1 : n1 + 1, half : half + WB, :] = total.reshape(n1, WB, 256).astype(BF16)
        parts = total.reshape(n1, 2, half, 256)
        even = parts[:, 0].reshape(n1 * half, 256)
        odd = parts[:, 1].reshape(n1 * half, 256)
        before = jnp.where(step == 0, 0.0, pltpu.roll(odd, 1, 0))
        after = jnp.where(step == half - 1, 0.0, pltpu.roll(even, n1 * half - 1, 0))
        ref[1 : n1 + 1, 0:half, :] = before.reshape(n1, half, 256).astype(BF16)
        ref[1 : n1 + 1, half + WB :, :] = after.reshape(n1, half, 256).astype(BF16)

    lane = iota((n1, half, 128), 2)
    blank = jnp.zeros((n1, half, 128), BF16)

    def turned(slab, block):
        if not 0 <= block < 2 * groups:
            return blank
        g, part = divmod(block, 2)
        values = h1_refs[g][1 : n1 + 1, slab * half : (slab + 1) * half, part * 128 : (part + 1) * 128]
        return pltpu.roll(values.reshape(n1 * half, 128), 96 if slab % 2 else 32, 1).reshape(n1, half, 128)

    def borders(g):
        for part in range(2):
            block = 2 * g + part
            for v in range(2):
                one, two = 2 * v, 2 * v + 1
                first = jnp.where(lane < 32, turned(one, block - 1), turned(one, block + 1))
                second = jnp.where(lane < 96, turned(two, block - 1), turned(two, block + 1))
                at = part * 256 + v * 128
                e_refs[g][1 : n1 + 1, :, at : at + 128] = jnp.where(lane < 64, first, second)

    def middle_layer(g):
        total = bias2
        for k in range(3):
            rows = pl.ds(off2 + k, n2)
            stack = []
            for part in range(2):
                parts = [
                    h1_refs[g][rows, o * half : (o + 1) * half, part * 128 : (part + 1) * 128] for o in range(4)
                ]
                parts.append(e_refs[g][rows, :, part * 256 : (part + 1) * 256])
                stack.append(jnp.concatenate([p.reshape(n2 * half, p.shape[2]) for p in parts], axis=1))
            total = total + dot_nt(jnp.concatenate(stack, axis=0), w2_ref[k])
        total = jnp.maximum(total, 0.0).reshape(2, n2, half, 256).astype(BF16)
        for part in range(2):
            for u in range(2):
                h2_refs[g][1 : n2 + 1, u * half : (u + 1) * half, part * 128 : (part + 1) * 128] = total[
                    part, :, :, u * 128 : (u + 1) * 128
                ]

    def last_layer(g):
        parts = []
        for k in range(3):
            cells_in = h2_refs[g][pl.ds(off3 + k, rows_here)].reshape(rows_here * WB, 256)
            parts.append(dot_nt(cells_in, w3_ref[k, :, g * 256 : (g + 1) * 256]))
        return sum(parts)

    for g in range(groups):
        first_layer(g)
    for g in range(groups):
        borders(g)
    for g in range(groups):
        middle_layer(g)
    total = sum(last_layer(g) for g in range(groups))
    for r in range(rows_here):
        for u in range(2):
            piece = total[(r * 2 + u) * half : (r * 2 + u + 1) * half]
            ya_ref[pl.ds(r * WB + u, half, stride=2), :] = piece[:, :128]
            yb_ref[pl.ds(r * WB + u, half, stride=2), :] = piece[:, 128:]
    here = rows_here * WB
    for v in range(here // 128):
        yt_ref[v, 0:128, :] = ya_ref[v * 128 : (v + 1) * 128, :].T
        yt_ref[v, 128:256, :] = yb_ref[v * 128 : (v + 1) * 128, :].T
    lane = iota((WA, here), 1)
    keep = (rows_here * trow + lane // WB).astype(F32) < count[:, :1]
    for ra in range(2):
        parts = [
            jnp.concatenate([yt_ref[v, pl.ds(l * 2 + ra, WA, stride=8), :] for v in range(here // 128)], axis=1)
            for l in range(3)
        ]
        before = jnp.where(lane % WB == 0, 0.0, pltpu.roll(parts[0], 1, 1))
        after = jnp.where(lane % WB == WB - 1, 0.0, pltpu.roll(parts[2], here - 1, 1))
        result = before + parts[1] + after + rest_ref[0:1, :1]
        out_ref[0, ra * WA : (ra + 1) * WA, :] = jnp.where(keep, result, 0.0)


def per_device(
    query_bank, ref_owner, target_feat, valid_rows, w_first, b_first, w_middle, b_middle, w_last, b_last
):
    target = target_feat[0]
    cells, width = target.shape
    positions = query_bank.shape[1]
    ch = w_middle.shape[0]
    group = 2 * ch
    lanes = WA * group
    trows = lax.axis_size("trow")
    grid_rows = cells // WB
    rows_here = grid_rows // trows
    sides = 1 if trows == 2 else 2
    n1, n2 = min(rows_here + 2 * sides, grid_rows), min(rows_here + sides, grid_rows)

    expand = pl.pallas_call(
        functools.partial(expand_kernel, ch),
        out_shape=(
            jax.ShapeDtypeStruct((3, lanes, 256), BF16),
            jax.ShapeDtypeStruct((3, 256, 768), BF16),
            jax.ShapeDtypeStruct((3, 256, lanes), BF16),
            jax.ShapeDtypeStruct((8, 256), F32),
        ),
        in_specs=[VMEM] * 3 + [HBM] * 2,
        out_specs=(VMEM,) * 4,
        scratch_shapes=[
            pltpu.SMEM((ch,), F32),
            pltpu.SMEM((ch,), F32),
            pltpu.SemaphoreType.DMA((2,)),
        ],
        compiler_params=pltpu.CompilerParams(vmem_limit_bytes=VMEM_LIMIT),
        name="expand",
    )
    weights = (
        jnp.transpose(w_first, (1, 2, 3, 4, 5, 0)).reshape(27, 3, ch),
        jnp.transpose(w_middle, (2, 3, 4, 5, 0, 1)).reshape(81, ch, ch),
        jnp.transpose(w_last, (0, 2, 3, 4, 5, 1)).reshape(27, 3, ch),
    )
    biased = lambda *taps: expand(*taps, in_hbm(b_first), in_hbm(b_middle))
    own, sibling, other, (w1, w2, w3, rows), rest = spread(
        query_bank[0], ref_owner, "pair", target, weights, biased, (b_last, valid_rows)
    )
    return pl.pallas_call(
        functools.partial(score_kernel, rows_here, n1, n2),
        out_shape=jax.ShapeDtypeStruct((1, positions, rows_here * WB), F32),
        in_specs=[VMEM] * 9,
        out_specs=VMEM,
        scratch_shapes=[
            pltpu.VMEM((8 + (grid_rows + 2) * PITCH, 128), F32),
            pltpu.VMEM((n1 + 2, WB, 256), BF16),
            pltpu.VMEM((rows_here * WB + 8, 128), F32),
            pltpu.VMEM((rows_here * WB + 8, 128), F32),
            pltpu.VMEM((rows_here * WB // 128, 256 + 8, 128), F32),
            *[pltpu.VMEM((n1 + 2, 2 * WB, 256), BF16)] * (lanes // 256),
            *[pltpu.VMEM((n1 + 2, WB // 2, 512), BF16)] * (lanes // 256),
            *[pltpu.VMEM((n2 + 2, WB, 256), BF16)] * (lanes // 256),
        ],
        compiler_params=pltpu.CompilerParams(vmem_limit_bytes=VMEM_LIMIT),
        name="score",
    )(rest, rows, target, other, own, sibling, w1, w2, w3)


def solution(mesh):
    in_specs = (
        P("pair", None, None),
        P(),
        P("pair", None, "trow"),
        P("pair"),
        P(),
        P(),
        P(),
        P(),
        P(),
        P(),
    )
    out_specs = P("pair", None, "trow")
    return jax.shard_map(per_device, mesh=mesh, in_specs=in_specs, out_specs=out_specs, check_vma=False)
```

```python
import functools
import math

import jax
import jax.numpy as jnp
from jax import lax
from jax.experimental import pallas as pl
from jax.experimental.pallas import tpu as pltpu
from jax.sharding import PartitionSpec as P

WB = 32
WA = 32

EPS_NORM = 1e-06
EPS_PEAK = 1e-05

F32 = jnp.float32
BF16 = jnp.bfloat16
NT = (((1,), (1,)), ((), ()))
PITCH = WB + 8
VMEM_LIMIT = 16 * 1024 * 1024
VMEM = pl.BlockSpec(memory_space=pltpu.VMEM)
SMEM = pl.BlockSpec(memory_space=pltpu.SMEM)
HBM = pl.BlockSpec(memory_space=pltpu.HBM)


def swapped(values, axis, distance):
    count = lax.axis_size(axis)
    return lax.ppermute(values, axis, [(i, i ^ distance) for i in range(count)])


def fetch_kernel(wf_hbm, wm_hbm, wl_hbm, wf_ref, wm_ref, wl_ref, sems):
    pairs = ((wf_hbm, wf_ref), (wm_hbm, wm_ref), (wl_hbm, wl_ref))
    copies = [pltpu.make_async_copy(src, dst, sems.at[n]) for n, (src, dst) in enumerate(pairs)]
    for copy in copies:
        copy.start()
    for copy in copies:
        copy.wait()


def front_kernel(axis, window_hbm, mine_ref, sem):
    half = mine_ref.shape[0]
    rows = pl.ds(pl.multiple_of(lax.axis_index(axis) % 2 * half, half), half)
    copy = pltpu.make_async_copy(window_hbm.at[rows], mine_ref, sem)
    copy.start()
    copy.wait()


def spread(window, owner, axis, target, weights, expand, rest):
    count = lax.axis_size(axis)
    rank = lax.axis_index(axis)
    half = window.shape[0] // 2
    theirs = swapped(window, axis, 1)
    fetch = pl.pallas_call(
        fetch_kernel,
        out_shape=[jax.ShapeDtypeStruct(w.shape, w.dtype) for w in weights],
        in_specs=[HBM] * 3,
        out_specs=[VMEM] * 3,
        scratch_shapes=[pltpu.SemaphoreType.DMA((3,))],
        compiler_params=pltpu.CompilerParams(vmem_limit_bytes=VMEM_LIMIT),
        name="fetch",
    )
    mine = pl.pallas_call(
        functools.partial(front_kernel, axis),
        out_shape=jax.ShapeDtypeStruct((half, window.shape[1]), window.dtype),
        in_specs=[HBM],
        out_specs=VMEM,
        scratch_shapes=[pltpu.SemaphoreType.DMA],
        compiler_params=pltpu.CompilerParams(vmem_limit_bytes=VMEM_LIMIT),
        name="front",
    )(in_hbm(window))
    mine, target, owner = lax.optimization_barrier((mine, target, owner))
    other = swapped(target, "trow", 1)
    owner = owner[0]
    theirs = lax.dynamic_slice_in_dim(theirs, rank % 2 * half, half, 0)
    sibling = owner + 1 - 2 * (owner % 2)
    held = jnp.where(rank == owner, mine, jnp.where(rank == sibling, theirs, jnp.zeros_like(mine)))
    held, weights = lax.optimization_barrier((held, weights))
    weights = fetch(*(in_hbm(w) for w in weights))
    bits = [1 << b for b in range(1, count.bit_length() - 1)]
    rounds = [bits[at : at + 2] for at in range(0, len(bits), 2)]
    for n, near in enumerate(rounds):
        distances = near if len(near) == 1 else [sum(near), *near[::-1]]
        held = held + sum(swapped(held, axis, d) for d in distances)
        if n == 0:
            held, weights, rest = lax.optimization_barrier((held, weights, rest))
            expanded = expand(*weights)
    b_last, valid_rows = rest
    rest = jnp.where(iota((8, 128), 0) == 0, b_last[0], valid_rows[0].astype(F32))
    held, rest, expanded = lax.optimization_barrier((held, rest, expanded))
    return held, swapped(held, axis, 1), other, expanded, rest


def in_hbm(array):
    return pltpu.with_memory_space_constraint(array, pltpu.HBM)


def dot(left, right):
    return jnp.dot(left, right, preferred_element_type=F32)


def dot_nt(left, right):
    return lax.dot_general(left, right, NT, preferred_element_type=F32)


def iota(shape, dim):
    return lax.broadcasted_iota(jnp.int32, shape, dim)


def one_hot(cond):
    return jnp.where(cond, 1.0, 0.0).astype(BF16)


def expand_kernel(
    ch, wf_ref, wm_ref, wl_ref, b1_hbm, b2_hbm, w1_ref, w2_ref, w3_ref, rows_ref, b1_ref, b2_ref, sems
):
    group = 2 * ch
    pairs = ((b1_hbm, b1_ref), (b2_hbm, b2_ref))
    copies = [pltpu.make_async_copy(src, dst, sems.at[n]) for n, (src, dst) in enumerate(pairs)]
    for copy in copies:
        copy.start()

    def by_offset(ref):
        values = ref[...].astype(F32)
        fill = jnp.zeros((32 - values.shape[0], ch), F32)
        return jnp.concatenate([part for l in range(3) for part in (values[:, l, :], fill)], axis=0)

    taps = by_offset(wf_ref)
    taps = jnp.concatenate([taps, jnp.zeros((32, ch), F32)], axis=0)
    taps = jnp.concatenate([taps, jnp.zeros((128, 128 - ch), F32)], axis=1).T[:ch].astype(BF16)
    lane = iota((128, 128), 1)
    src = iota((128, 128), 0)
    base = []
    for k in range(3):
        for ra in range(2):
            l, rp, j = lane // 6, (lane // 3) % 2, lane % 3
            want = l * 32 + ((rp - ra + 1) * 3 + j) * 3 + k
            base.append(dot(taps, one_hot((src == want) & (lane < 18))))
    base = jnp.concatenate(base, axis=0).astype(BF16)[:, :32]
    row = iota((32, 256), 0)
    col = iota((32, 256), 1)
    l, rp, j = row // 6, (row // 3) % 2, row % 3
    for ca in range(WA):
        at = ca + j - 1
        place = one_hot((col == l * 64 + rp * WA + at) & (at >= 0) & (at < WA) & (row < 18))
        block = dot(base, place).astype(BF16)
        for k in range(3):
            w1_ref[k, ca * group : (ca + 1) * group, :] = block[k * group : (k + 1) * group]

    total = None
    row = iota((ch, 128), 0)
    col = iota((ch, 128), 1)
    for j in range(3):
        for rp in range(2):
            picked = jnp.concatenate(
                [wm_ref[(((rp - ra + 1) * 3 + j) * 3 + k) * 3 + l] for k in range(3) for l in range(3) for ra in range(2)],
                axis=0,
            )
            part = dot(picked, one_hot(col == j * group + rp * ch + row))
            total = part if total is None else total + part
    base = total.astype(BF16)
    row = iota((128, 128), 0)
    col = iota((128, 128), 1)
    inner = [dot(base, one_hot((col == row + group * (ca - 1)) & (row < 3 * group))).astype(BF16) for ca in range(4)]
    outer = {
        (side, half): dot(
            base, one_hot((col == row + half * 64 + (-group if side else 0)) & (row // group == 2 * side))
        ).astype(BF16)
        for side in range(2)
        for half in range(2)
    }
    left = iota((group, 128), 1) < 64
    blank = jnp.zeros((group, 128), BF16)
    for k in range(3):
        tap = lambda values, l: values[(k * 3 + l) * group : (k * 3 + l + 1) * group] if 0 <= l < 3 else blank
        for u in range(2):
            for ca in range(4):
                rows = slice((u * 4 + ca) * group, (u * 4 + ca + 1) * group)
                for slab in range(4):
                    w2_ref[k, rows, slab * 128 : (slab + 1) * 128] = tap(inner[ca], slab - u)
                for v in range(2):
                    piece = blank
                    if ca in (0, 3):
                        side = ca // 3
                        piece = jnp.where(left, tap(outer[side, 0], 2 * v - u), tap(outer[side, 1], 2 * v + 1 - u))
                    w2_ref[k, rows, 512 + v * 128 : 640 + v * 128] = piece

    taps = by_offset(wl_ref).astype(BF16)
    out_row = iota((24, 96), 0)
    src = iota((24, 96), 1)
    row = iota((ch, 128), 0)
    col = iota((ch, 128), 1)
    total = None
    for j in range(3):
        for rp in range(2):
            k, l, ra = out_row // 8, (out_row % 8) // 2, out_row % 2
            want = l * 32 + ((rp - ra + 1) * 3 + j) * 3 + k
            picked = dot(one_hot((src == want) & (l < 3)), taps).astype(BF16)
            part = dot(picked, one_hot(col == j * group + rp * ch + row))
            total = part if total is None else total + part
    base = total.astype(BF16)
    row = iota((128, 256), 0)
    col = iota((128, 256), 1)
    moved = [dot(base, one_hot((col == row + group * b) & (row < 3 * group))) for b in range(4)]
    blank = jnp.zeros((8, 128), F32)
    lanes = WA * group // 128
    for k in range(3):
        for pair in range(WA // 2):
            for v in range(lanes):
                chunks = []
                for ca in (2 * pair, 2 * pair + 1):
                    a, b = (ca - 1) // 4, (ca - 1) % 4
                    piece = moved[b][k * 8 : (k + 1) * 8]
                    chunks.append(piece[:, :128] if v == a else piece[:, 128:] if v == a + 1 else blank)
                w3_ref[k, pair * 16 : (pair + 1) * 16, v * 128 : (v + 1) * 128] = jnp.concatenate(
                    chunks, axis=0
                ).astype(BF16)

    for copy in copies:
        copy.wait()

    chan = iota((1, 256), 1) % ch
    for n, ref in enumerate((b1_ref, b2_ref)):
        total = jnp.zeros((1, 256), F32)
        for o in range(ch):
            total = jnp.where(chan == o, ref[o], total)
        rows_ref[n : n + 1, :] = total


def score_kernel(
    rows_here, n1, n2, rest_ref, rows_ref, tm_ref, to_ref, qa_ref, qb_ref, w1_ref, w2_ref, w3_ref,
    out_ref, v_ref, x_ref, ya_ref, yb_ref, yt_ref, o_ref, sems, *layers,
):
    trow, bit = lax.axis_index("trow"), lax.axis_index("pair") % 2
    count = rest_ref[1:2, :]
    cells = tm_ref.shape[0]
    grid_rows = cells // WB
    width = tm_ref.shape[1]
    scale = math.sqrt(2 * width)
    start1 = jnp.clip(rows_here * trow - 2, 0, grid_rows - n1)
    start2 = jnp.clip(rows_here * trow - 1, 0, grid_rows - n2)

    def unit(ref):
        values = ref[...].astype(F32)
        return (values * lax.rsqrt(jnp.sum(values * values, axis=1, keepdims=True) + EPS_NORM)).astype(BF16)

    qa, qb = unit(qa_ref), unit(qb_ref)
    own_first = bit == 0
    q0 = jnp.where(own_first, qa, qb)
    q1 = jnp.where(own_first, qb, qa)
    query = jnp.concatenate([q0, q1, q0, q1], axis=0)
    low, high = query[:, :width], query[:, width:]
    near = jnp.where(trow == 0, low, high)
    far = jnp.where(trow == 0, high, low)
    raw = dot_nt(tm_ref[...], near) + dot_nt(to_ref[...], far)

    def squares(ref):
        values = ref[...].astype(F32)
        return jnp.sum(values * values, axis=1, keepdims=True)

    inv = lax.rsqrt(squares(tm_ref) + squares(to_ref) + EPS_NORM)
    live = (iota((cells, 128), 0) // WB).astype(F32) < count
    corr = jnp.where(live, scale * raw * inv, 0.0)
    mag = jnp.abs(corr)
    peak_query = jnp.max(mag, axis=1, keepdims=True)
    peak_target = jnp.max(mag, axis=0, keepdims=True)
    volume = corr * (corr * (1.0 / (peak_query + EPS_PEAK))) * (corr * (1.0 / (peak_target + EPS_PEAK)))

    v_ref[0 : 8 + PITCH, :] = jnp.zeros((8 + PITCH, 128), F32)
    v_ref[8 + (grid_rows + 1) * PITCH :, :] = jnp.zeros((PITCH, 128), F32)
    for r in range(grid_rows):
        at = 8 + (r + 1) * PITCH
        v_ref[at : at + WB, :] = volume[r * WB : (r + 1) * WB]
        v_ref[at + WB : at + PITCH, :] = jnp.zeros((PITCH - WB, 128), F32)

    half = WB // 2
    left = iota((half, 128), 1) < 64
    for r in range(n1 + 2):
        at = pl.multiple_of((start1 + r) * PITCH, 8)
        slabs = [v_ref[pl.ds(at + 8 + o, half, stride=2), :] for o in (-1, 0, 1, 2)]
        for u in range(2):
            x_ref[r, u * half : (u + 1) * half, 0:128] = jnp.where(left, slabs[u], slabs[u + 1]).astype(BF16)
            x_ref[r, u * half : (u + 1) * half, 128:256] = jnp.where(left, slabs[u + 2], 0.0).astype(BF16)

    groups = len(layers) // 3
    h1_refs, e_refs, h2_refs = layers[:groups], layers[groups : 2 * groups], layers[2 * groups :]
    for ref, count1 in [(r, n1) for r in (*h1_refs, *e_refs)] + [(r, n2) for r in h2_refs]:
        ref[0] = jnp.zeros(ref.shape[1:], BF16)
        ref[count1 + 1] = jnp.zeros(ref.shape[1:], BF16)
    bias1, bias2 = rows_ref[0:1, :], rows_ref[1:2, :]
    off2 = start2 - start1
    off3 = rows_here * trow - start2
    step = iota((n1 * half, 256), 0) % half

    def first_layer(g):
        cols = slice(g * 256, (g + 1) * 256)
        total = bias1
        for k in range(3):
            total = total + dot_nt(x_ref[k : k + n1].reshape(n1 * WB, 256), w1_ref[k, cols, :])
        total = jnp.maximum(total, 0.0)
        ref = h1_refs[g]
        ref[1 : n1 + 1, half : half + WB, :] = total.reshape(n1, WB, 256).astype(BF16)
        parts = total.reshape(n1, 2, half, 256)
        even = parts[:, 0].reshape(n1 * half, 256)
        odd = parts[:, 1].reshape(n1 * half, 256)
        before = jnp.where(step == 0, 0.0, pltpu.roll(odd, 1, 0))
        after = jnp.where(step == half - 1, 0.0, pltpu.roll(even, n1 * half - 1, 0))
        ref[1 : n1 + 1, 0:half, :] = before.reshape(n1, half, 256).astype(BF16)
        ref[1 : n1 + 1, half + WB :, :] = after.reshape(n1, half, 256).astype(BF16)

    lane = iota((n1, half, 128), 2)
    blank = jnp.zeros((n1, half, 128), BF16)

    def turned(slab, block):
        if not 0 <= block < 2 * groups:
            return blank
        g, part = divmod(block, 2)
        values = h1_refs[g][1 : n1 + 1, slab * half : (slab + 1) * half, part * 128 : (part + 1) * 128]
        return pltpu.roll(values.reshape(n1 * half, 128), 96 if slab % 2 else 32, 1).reshape(n1, half, 128)

    def borders(g):
        for part in range(2):
            block = 2 * g + part
            for v in range(2):
                one, two = 2 * v, 2 * v + 1
                first = jnp.where(lane < 32, turned(one, block - 1), turned(one, block + 1))
                second = jnp.where(lane < 96, turned(two, block - 1), turned(two, block + 1))
                at = part * 256 + v * 128
                e_refs[g][1 : n1 + 1, :, at : at + 128] = jnp.where(lane < 64, first, second)

    def middle_layer(g):
        total = bias2
        for k in range(3):
            rows = pl.ds(off2 + k, n2)
            stack = []
            for part in range(2):
                parts = [
                    h1_refs[g][rows, o * half : (o + 1) * half, part * 128 : (part + 1) * 128] for o in range(4)
                ]
                parts.append(e_refs[g][rows, :, part * 256 : (part + 1) * 256])
                stack.append(jnp.concatenate([p.reshape(n2 * half, p.shape[2]) for p in parts], axis=1))
            total = total + dot_nt(jnp.concatenate(stack, axis=0), w2_ref[k])
        total = jnp.maximum(total, 0.0).reshape(2, n2, half, 256).astype(BF16)
        for part in range(2):
            for u in range(2):
                h2_refs[g][1 : n2 + 1, u * half : (u + 1) * half, part * 128 : (part + 1) * 128] = total[
                    part, :, :, u * 128 : (u + 1) * 128
                ]

    def last_layer(g):
        parts = []
        for k in range(3):
            cells_in = h2_refs[g][pl.ds(off3 + k, rows_here)].reshape(rows_here * WB, 256)
            parts.append(dot_nt(cells_in, w3_ref[k, :, g * 256 : (g + 1) * 256]))
        return sum(parts)

    for g in range(groups):
        first_layer(g)
    for g in range(groups):
        borders(g)
    for g in range(groups):
        middle_layer(g)
    total = sum(last_layer(g) for g in range(groups))
    for r in range(rows_here):
        for u in range(2):
            piece = total[(r * 2 + u) * half : (r * 2 + u + 1) * half]
            ya_ref[pl.ds(r * WB + u, half, stride=2), :] = piece[:, :128]
            yb_ref[pl.ds(r * WB + u, half, stride=2), :] = piece[:, 128:]
    here = rows_here * WB
    for v in range(here // 128):
        yt_ref[v, 0:128, :] = ya_ref[v * 128 : (v + 1) * 128, :].T
        yt_ref[v, 128:256, :] = yb_ref[v * 128 : (v + 1) * 128, :].T
    copies = []
    lane = iota((WA, here), 1)
    keep = (rows_here * trow + lane // WB).astype(F32) < count[:, :1]
    for ra in range(2):
        parts = [
            jnp.concatenate([yt_ref[v, pl.ds(l * 2 + ra, WA, stride=8), :] for v in range(here // 128)], axis=1)
            for l in range(3)
        ]
        before = jnp.where(lane % WB == 0, 0.0, pltpu.roll(parts[0], 1, 1))
        after = jnp.where(lane % WB == WB - 1, 0.0, pltpu.roll(parts[2], here - 1, 1))
        result = before + parts[1] + after + rest_ref[0:1, :1]
        rows = slice(ra * WA, (ra + 1) * WA)
        o_ref[rows, :] = jnp.where(keep, result, 0.0)
        copies.append(pltpu.make_async_copy(o_ref.at[rows], out_ref.at[0, rows], sems.at[ra]))
        copies[-1].start()
    for copy in copies:
        copy.wait()


def per_device(
    query_bank, ref_owner, target_feat, valid_rows, w_first, b_first, w_middle, b_middle, w_last, b_last
):
    target = target_feat[0]
    cells, width = target.shape
    positions = query_bank.shape[1]
    ch = w_middle.shape[0]
    group = 2 * ch
    lanes = WA * group
    trows = lax.axis_size("trow")
    grid_rows = cells // WB
    rows_here = grid_rows // trows
    sides = 1 if trows == 2 else 2
    n1, n2 = min(rows_here + 2 * sides, grid_rows), min(rows_here + sides, grid_rows)

    expand = pl.pallas_call(
        functools.partial(expand_kernel, ch),
        out_shape=(
            jax.ShapeDtypeStruct((3, lanes, 256), BF16),
            jax.ShapeDtypeStruct((3, 256, 768), BF16),
            jax.ShapeDtypeStruct((3, 256, lanes), BF16),
            jax.ShapeDtypeStruct((8, 256), F32),
        ),
        in_specs=[VMEM] * 3 + [HBM] * 2,
        out_specs=(VMEM,) * 4,
        scratch_shapes=[
            pltpu.SMEM((ch,), F32),
            pltpu.SMEM((ch,), F32),
            pltpu.SemaphoreType.DMA((2,)),
        ],
        compiler_params=pltpu.CompilerParams(vmem_limit_bytes=VMEM_LIMIT),
        name="expand",
    )
    weights = (
        jnp.transpose(w_first, (1, 2, 3, 4, 5, 0)).reshape(27, 3, ch),
        jnp.transpose(w_middle, (2, 3, 4, 5, 0, 1)).reshape(81, ch, ch),
        jnp.transpose(w_last, (0, 2, 3, 4, 5, 1)).reshape(27, 3, ch),
    )
    biased = lambda *taps: expand(*taps, in_hbm(b_first), in_hbm(b_middle))
    own, sibling, other, (w1, w2, w3, rows), rest = spread(
        query_bank[0], ref_owner, "pair", target, weights, biased, (b_last, valid_rows)
    )
    return pl.pallas_call(
        functools.partial(score_kernel, rows_here, n1, n2),
        out_shape=jax.ShapeDtypeStruct((1, positions, rows_here * WB), F32),
        in_specs=[VMEM] * 9,
        out_specs=HBM,
        scratch_shapes=[
            pltpu.VMEM((8 + (grid_rows + 2) * PITCH, 128), F32),
            pltpu.VMEM((n1 + 2, WB, 256), BF16),
            pltpu.VMEM((rows_here * WB + 8, 128), F32),
            pltpu.VMEM((rows_here * WB + 8, 128), F32),
            pltpu.VMEM((rows_here * WB // 128, 256 + 8, 128), F32),
            pltpu.VMEM((positions, rows_here * WB), F32),
            pltpu.SemaphoreType.DMA((2,)),
            *[pltpu.VMEM((n1 + 2, 2 * WB, 256), BF16)] * (lanes // 256),
            *[pltpu.VMEM((n1 + 2, WB // 2, 512), BF16)] * (lanes // 256),
            *[pltpu.VMEM((n2 + 2, WB, 256), BF16)] * (lanes // 256),
        ],
        compiler_params=pltpu.CompilerParams(vmem_limit_bytes=VMEM_LIMIT),
        name="score",
    )(rest, rows, target, other, own, sibling, w1, w2, w3)


def solution(mesh):
    in_specs = (
        P("pair", None, None),
        P(),
        P("pair", None, "trow"),
        P("pair"),
        P(),
        P(),
        P(),
        P(),
        P(),
        P(),
    )
    out_specs = P("pair", None, "trow")
    return jax.shard_map(per_device, mesh=mesh, in_specs=in_specs, out_specs=out_specs, check_vma=False)
```
